128 devices in a mesh: wide: 32 (over x, y_lo, z), narrow: 4 (over y_hi, core).
Axes of the slice: x: 4, y: 4 (y_hi: 2, y_lo: 2; y = y_hi * 2 + y_lo), z: 4, core: 2. Of those that a mesh axis runs over, the one named last changes fastest.
Arguments:
- hidden: bfloat16 [2048, 4096], P('narrow', 'wide'), may hold values from -6 to 6
- attn_gain: float32 [4096], replicated, may hold values from 0.5 to 1.5
- query_weight: bfloat16 [4096, 4096], P(None, 'wide'), may hold values from -0.09375 to 0.09375
- key_weight: bfloat16 [4096, 1024], P('wide'), may hold values from -0.1875 to 0.1875
- value_weight: bfloat16 [4096, 1024], P('wide'), may hold values from -0.1875 to 0.1875
- out_weight: bfloat16 [4096, 4096], P('wide'), may hold values from -0.09375 to 0.09375
- cache_key: bfloat16 [8, 512, 128], replicated, may hold values from -600 to 600
- cache_value: bfloat16 [8, 512, 128], replicated, may hold values from -6 to 6
- mlp_gain: float32 [4096], replicated, may hold values from 0.5 to 1.5
- router_weight: bfloat16 [4096, 16], replicated, may hold values from -0.09375 to 0.09375
- expert_ids: int32 [2048, 2], P('narrow'), may hold values from 0 to 15, all different within a row; in each aligned block of 16 rows (0 to 15, 16 to 31, ...) at most 4 rows name the same one
- gate_weight: bfloat16 [32, 4096, 3200], P('wide', None, 'narrow'), may hold values from -0.09375 to 0.09375
- up_weight: bfloat16 [32, 4096, 3200], P('wide', None, 'narrow'), may hold values from -0.09375 to 0.09375
- down_weight: bfloat16 [32, 3200, 4096], P('wide', 'narrow'), may hold values from -0.078125 to 0.078125
Outputs:
- layer_out: bfloat16 [2048, 4096], P('narrow', 'wide')
The draws below stay inside these ranges and needn't reach their ends.
Inputs may be any that keep to these rules, and one draw needn't show every extreme that they name: `expert_ids`: in each aligned block of 16 rows no expert is named by more than 4 rows, and in every block some expert by exactly 4; the two experts of a row differ.
All inputs are finite; a program needn't handle non-finite values.
Results may differ from the reference program's by a relative error of at most 0.012.
The reference program's roundings to bfloat16 on the way count: a program that leaves them out, or rounds other values in their place, can miss the bound.
Values may be sent and summed in bfloat16 or wider, within the bound.
A program may use at most 128 MiB of HBM per device.

```python
import math
import jax
import jax.numpy as jnp
import numpy as np
from jax import lax

D = 4096
HEADS = 32
KV_HEADS = 8
HEAD_DIM = 128
FF = 6400
EXPERTS = 16
SPLIT = 2
TOK_BLOCK = 16
CTX = 512
SPAN = 2048
CAPD = 4
SLOTS = 32


def draw_cache_key(key, part):
    base = jax.random.normal(key, (KV_HEADS, CTX, HEAD_DIM), jnp.float32)
    return jnp.clip(base, -600.0, 600.0).astype(jnp.bfloat16)


def with_spikes(array, stream_key, source, target, blocks, factor):
    owner, partner = [(jnp.arange(array.shape[dim]) // (array.shape[dim] // blocks)).reshape([-1 if axis == dim else 1 for axis in range(array.ndim)]) for dim in (source, target)]
    chosen = jax.random.permutation(stream_key, blocks)[partner]
    strong = (owner == chosen) | (owner == (partner + blocks // 2) % blocks)
    return jnp.where(strong, factor * array, array)


def level_of(key, dims, cuts, low, high):
    def one(axis_at, shards_of):
        heights = jax.random.uniform(jax.random.fold_in(jax.random.fold_in(key, 6), axis_at), (shards_of,), jnp.float32, low / len(cuts), high / len(cuts))
        return jnp.repeat(jnp.exp(heights), dims[axis_at] // shards_of).reshape((-1,) + (1,) * (len(dims) - axis_at - 1))

    level = one(*cuts[0])
    for cut in cuts[1:]:
        level = level * one(*cut)
    return level


def deal_out(own_key, own, number, rows, count, top, reach, slope):
    sequence = jax.random.permutation(own_key, count)
    heavy_load, common = shares(count, rows * top, reach, slope, True), shares(count, rows * top, reach, slope, False)
    places = jnp.arange(count)

    def named(lengths, offset_by):
        used = int((lengths > 0).sum())
        fixed = max(1, used // 4)
        shifted = fixed + (places - fixed + offset_by * (used - fixed)) % max(1, count - fixed)
        return jnp.zeros((count,), jnp.int32).at[sequence[jnp.where(places < fixed, places, shifted)]].set(jnp.asarray(lengths, jnp.int32))

    lengths = jnp.where(number % 4 == 0, named(heavy_load, number // 4), named(common, number - number // 4 - 1))
    mixed = jax.random.permutation(jax.random.fold_in(own, 3), count)
    source_of, sink = mixed[0:count // 2 * 2:2], mixed[1:count // 2 * 2:2]
    slack = jnp.minimum(lengths[source_of] - 1, reach - lengths[sink]) // 2
    slack = jnp.where((source_of == sequence[0]) | (sink == sequence[0]) | (lengths[sink] == 0), 0, jnp.maximum(slack, 0))
    shifted = jax.random.randint(jax.random.fold_in(own, 4), (count // 2,), 0, 1 << 20) % (slack + 1)
    lengths = lengths.at[source_of].add(-shifted).at[sink].add(shifted)
    labels = jnp.searchsorted(jnp.cumsum(lengths), jnp.arange(rows * top), side="right").astype(jnp.int32)
    grid = labels.reshape(top, rows).T
    grid = grid[jax.random.permutation(jax.random.fold_in(own, 1), rows)]
    offset_by = jax.random.randint(jax.random.fold_in(own, 2), (rows, 1), 0, top)
    return jnp.take_along_axis(grid, (jnp.arange(top)[None, :] + offset_by) % top, axis=1)


def shares(count, total, limit, slope, full):
    weights = [(1 << 20) // math.isqrt(standing ** slope) + 1 for standing in range(1, count + 1)]
    largest = limit if full else min(limit, max(-(-total // count), total * weights[0] // sum(weights)))
    least = 1 if total - largest >= count - 1 else 0
    given, surplus = [largest] + [least] * (count - 1), total - largest - least * (count - 1)
    while surplus > 0:
        candidates = [i for i in range(1, count) if given[i] < largest] or [i for i in range(1, count) if given[i] < limit]
        mass, remaining = sum([weights[i] for i in candidates]), surplus
        for i in candidates:
            addition = min(limit - given[i], max(1, remaining * weights[i] // mass), surplus)
            given[i] = given[i] + addition
            surplus = surplus - addition
    return np.array(given)


def normal_values(rng, extent, deviation, bound, pieces=(), kind=jnp.bfloat16):
    values = jax.random.normal(rng, extent, jnp.float32) * deviation
    if len(pieces) > 0:
        values = level_of(rng, extent, pieces, -0.22, 0.18) * values
    return jnp.clip(values, min=-bound, max=bound).astype(kind)


def bell_draw_with(rng, extent, spread, limit, shards, heavy, kind=jnp.bfloat16):
    entries = spread * jax.random.normal(rng, extent, jnp.float32)
    if shards:
        entries = entries * level_of(rng, extent, shards, -0.22, 0.18)
    return jnp.clip(with_spikes(entries, jax.random.fold_in(rng, 3), *heavy), -limit, limit).astype(kind)


def setup_inputs(seed: int = 0) -> dict:
    key_of = jax.random.split(jax.random.key(seed), 15)
    hidden = normal_values(key_of[0], (SPAN, D), 1.0, 6.0, ((0, 4), (1, 32)))
    attn_gain = jnp.clip(1.0 + 0.1 * jax.random.normal(key_of[1], (D,), jnp.float32), 0.5, 1.5)
    query_weight = normal_values(key_of[2], (D, HEADS * HEAD_DIM), D ** -0.5, 0.09375, ((1, 32),))
    key_weight = bell_draw_with(key_of[3], (D, KV_HEADS * HEAD_DIM), D ** -0.5, 0.1875, ((0, 32),), (0, 1, 32, 2.75))
    value_weight = bell_draw_with(key_of[4], (D, KV_HEADS * HEAD_DIM), D ** -0.5, 0.1875, ((0, 32),), (0, 1, 32, 2.75))
    out_weight = normal_values(key_of[5], (HEADS * HEAD_DIM, D), (HEADS * HEAD_DIM) ** -0.5, 0.09375, ((0, 32),))
    cache_key = draw_cache_key(jax.random.fold_in(key_of[14], 71), 0)
    cache_value = normal_values(key_of[7], (KV_HEADS, CTX, HEAD_DIM), 1.0, 6.0)
    mlp_gain = jnp.clip(1.0 + 0.1 * jax.random.normal(key_of[8], (D,), jnp.float32), 0.5, 1.5)
    router_weight = normal_values(key_of[9], (D, EXPERTS), D ** -0.5, 0.09375)
    expert_ids_keys = jax.random.split(jax.random.fold_in(key_of[10], 1), SPAN // TOK_BLOCK)
    expert_ids_turns = jax.random.permutation(jax.random.fold_in(key_of[10], 3), SPAN // TOK_BLOCK)
    expert_ids = jax.vmap(lambda own, number: deal_out(jax.random.fold_in(key_of[10], 2), own, number, TOK_BLOCK, EXPERTS, 2, CAPD, 2))(expert_ids_keys, expert_ids_turns).reshape((SPAN, 2))
    gate_weight = normal_values(key_of[11], (SLOTS, D, FF // SPLIT), D ** -0.5, 0.09375, ((0, 32), (2, 4)))
    up_weight = normal_values(key_of[12], (SLOTS, D, FF // SPLIT), D ** -0.5, 0.09375, ((0, 32), (2, 4)))
    down_weight = normal_values(key_of[13], (SLOTS, FF // SPLIT, D), FF ** -0.5, 0.078125, ((0, 32), (1, 4)))
    return dict(hidden=hidden, attn_gain=attn_gain, query_weight=query_weight, key_weight=key_weight, value_weight=value_weight, out_weight=out_weight, cache_key=cache_key, cache_value=cache_value, mlp_gain=mlp_gain, router_weight=router_weight, expert_ids=expert_ids, gate_weight=gate_weight, up_weight=up_weight, down_weight=down_weight)


epsilon = 1e-05

def layer_normed(values, gain):
    average = lax.optimization_barrier(jnp.mean(values, axis=-1, keepdims=True))
    centered = values - average
    variance = lax.optimization_barrier(jnp.mean(centered * centered, axis=-1, keepdims=True))
    return centered * lax.rsqrt(variance + epsilon) * gain

def slot_targets(routing, experts, capacity):
    blocks = routing.shape[0]
    flat_ids = routing.reshape(blocks, -1)
    onehot = (flat_ids[:, :, None] == jnp.arange(experts, dtype=jnp.int32)[None, None, :]).astype(jnp.int32)
    earlier = jnp.cumsum(onehot, axis=1) - onehot
    position = lax.optimization_barrier(jnp.sum(earlier * onehot, axis=2))
    return (flat_ids * capacity + position).reshape(routing.shape)

def fill_buffer(normed, target, slot_count):
    matches = (target[:, :, :, None] == jnp.arange(slot_count, dtype=jnp.int32)).astype(jnp.float32)
    placing = lax.optimization_barrier(jnp.sum(matches, axis=2))
    return jnp.einsum('btj,btd->bjd', placing, normed.astype(jnp.float32)).astype(jnp.bfloat16)

def pair_weights(logits, routing):
    picked = jnp.take_along_axis(logits, routing, axis=-1)
    leading = jax.nn.sigmoid(picked[..., 0] - picked[..., 1])
    return jnp.stack([leading, 1.0 - leading], axis=-1)

def gather_back(results, target, weights):
    blocks, slot_count = (results.shape[0], results.shape[1])
    flat_rows = results.reshape(blocks * slot_count, results.shape[2])
    row_index = target + (jnp.arange(blocks, dtype=jnp.int32) * slot_count)[:, None, None]
    picked = jnp.take(flat_rows, row_index.reshape(-1), axis=0).reshape(target.shape + (results.shape[2],))
    return lax.optimization_barrier(jnp.sum(picked * weights[..., None], axis=2))

def reference(hidden, attn_gain, query_weight, key_weight, value_weight, out_weight, cache_key, cache_value, mlp_gain, router_weight, expert_ids, gate_weight, up_weight, down_weight):
    share = HEADS // KV_HEADS
    normed = layer_normed(hidden.astype(jnp.float32), attn_gain).astype(jnp.bfloat16)
    queries = jnp.dot(normed, query_weight, preferred_element_type=jnp.float32).astype(jnp.bfloat16)
    fresh_keys = jnp.dot(normed, key_weight, preferred_element_type=jnp.float32).astype(jnp.bfloat16)
    fresh_values = jnp.dot(normed, value_weight, preferred_element_type=jnp.float32).astype(jnp.bfloat16)
    queries = queries.reshape(SPAN, HEADS, HEAD_DIM).transpose(1, 0, 2)
    fresh_keys = jnp.repeat(fresh_keys.reshape(SPAN, KV_HEADS, HEAD_DIM).transpose(1, 0, 2), share, axis=0)
    fresh_values = jnp.repeat(fresh_values.reshape(SPAN, KV_HEADS, HEAD_DIM).transpose(1, 0, 2), share, axis=0)
    old_keys_all = jnp.repeat(cache_key, share, axis=0)
    old_values_all = jnp.repeat(cache_value, share, axis=0)
    row_ids = jnp.arange(SPAN, dtype=jnp.int32)
    key_ids = jnp.arange(CTX + SPAN, dtype=jnp.int32) - CTX
    allowed = key_ids[None, :] <= row_ids[:, None]

    def one_head(items):
        head_query, old_keys, old_values, new_keys, new_values = items
        all_keys = jnp.concatenate([old_keys, new_keys], axis=0)
        all_values = jnp.concatenate([old_values, new_values], axis=0)
        scores = jnp.dot(head_query, all_keys.T, preferred_element_type=jnp.float32) * HEAD_DIM ** (-0.5)
        scores = jnp.where(allowed, scores, -1e+30)
        highest = lax.optimization_barrier(jnp.max(scores, axis=1, keepdims=True))
        weights = jnp.exp(scores - highest)
        weights = (weights / lax.optimization_barrier(jnp.sum(weights, axis=1, keepdims=True))).astype(jnp.bfloat16)
        return jnp.dot(weights, all_values, preferred_element_type=jnp.float32).astype(jnp.bfloat16)
    attended = lax.map(one_head, (queries, old_keys_all, old_values_all, fresh_keys, fresh_values))
    attended = attended.transpose(1, 0, 2).reshape(SPAN, HEADS * HEAD_DIM)
    head_mix = jnp.dot(attended, out_weight, preferred_element_type=jnp.float32)
    residual = (hidden.astype(jnp.float32) + head_mix).astype(jnp.bfloat16)
    normed_two = layer_normed(residual.astype(jnp.float32), mlp_gain).astype(jnp.bfloat16)
    logits = jnp.dot(normed_two, router_weight, preferred_element_type=jnp.float32)
    blocks = SPAN // TOK_BLOCK
    routing = expert_ids.reshape(blocks, TOK_BLOCK, 2)
    target = slot_targets(routing, EXPERTS, CAPD)
    buffer = fill_buffer(normed_two.reshape(blocks, TOK_BLOCK, D), target, EXPERTS * CAPD)
    buffer = buffer.reshape(blocks, EXPERTS, CAPD, D)

    def one_slot(items):
        slot_index, w_gate, w_up, w_down = items
        tokens_in = jnp.take(buffer, slot_index // SPLIT, axis=1).reshape(blocks * CAPD, D)
        gate_term = jnp.dot(tokens_in, w_gate, preferred_element_type=jnp.float32)
        up_term = jnp.dot(tokens_in, w_up, preferred_element_type=jnp.float32)
        active = (jax.nn.silu(gate_term) * up_term).astype(jnp.bfloat16)
        return jnp.dot(active, w_down, preferred_element_type=jnp.float32).astype(jnp.bfloat16).reshape(blocks, CAPD, D)
    slot_out = lax.map(one_slot, (jnp.arange(EXPERTS * SPLIT, dtype=jnp.int32), gate_weight, up_weight, down_weight))
    summed = lax.optimization_barrier(jnp.sum(slot_out.reshape(EXPERTS, SPLIT, blocks, CAPD, D).astype(jnp.float32), axis=1))
    summed = summed.transpose(1, 0, 2, 3).reshape(blocks, EXPERTS * CAPD, D)
    mixture = gather_back(summed, target, pair_weights(logits.reshape(blocks, TOK_BLOCK, EXPERTS), routing))
    return (residual.astype(jnp.float32) + mixture.reshape(SPAN, D)).astype(jnp.bfloat16)
```

```python
import jax
import jax.numpy as jnp
from jax import lax
from jax.experimental import pallas as pl
from jax.experimental.pallas import tpu as pltpu
from jax.sharding import PartitionSpec as P

MESH = pl.DeviceIdType.MESH
F32 = jnp.float32
BF16 = jnp.bfloat16

XN, YL, ZN = 4, 2, 4
WIDE = XN * YL * ZN
NARROW = 4
ROWS = 512
LANE = 128
D = WIDE * LANE
HALF = ROWS // 2
KV_SHARE = 4
EXPERTS = 16
CAP = 4
BLOCK = 16
HIDDEN = 800
EPS = 1e-5
SCALE = LANE**-0.5


def remote(src, dst, send_sem, recv_sem, wide, narrow):
    return pltpu.make_async_remote_copy(
        src_ref=src,
        dst_ref=dst,
        send_sem=send_sem,
        recv_sem=recv_sem,
        device_id=(wide, narrow),
        device_id_type=MESH,
    )


def wait_bytes(ref, sem):
    pltpu.make_async_copy(ref, ref, sem).wait()


def dot(a, b):
    return jnp.dot(a, b, preferred_element_type=F32)


def wide_of(x, y, z):
    return (x * YL + y) * ZN + z


class Spread:
    def __init__(self, own, buf, me, narrow, send_sem, recv_sem):
        self.own, self.buf, self.me, self.narrow = own, buf, me, narrow
        self.send_sem, self.recv_sem = send_sem, recv_sem
        self.x = me // (YL * ZN)
        self.y = (me // ZN) % YL
        self.z = me % ZN
        self.started = []

    def place(self, half, first, y, second):
        return wide_of(first, y, second) if half == 0 else wide_of(second, y, first)

    def coordinates(self, half):
        return (self.x, self.z) if half == 0 else (self.z, self.x)

    def send(self, half, block, target):
        rows = pl.ds(half * HALF, HALF)
        own = block is None
        slot = self.me if own else block
        copy = remote(
            self.own.at[rows] if own else self.buf.at[slot, rows],
            self.buf.at[slot, rows],
            self.send_sem.at[len(self.started)],
            self.recv_sem.at[half, slot],
            target,
            self.narrow,
        )
        copy.start()
        self.started.append(copy)

    def arrive(self, half, block):
        rows = pl.ds(half * HALF, HALF)
        wait_bytes(self.buf.at[block, rows], self.recv_sem.at[half, block])

    def around(self, half, block, dimension):
        first, second = self.coordinates(half)
        for step in (1, 3):
            if dimension == 0:
                target = self.place(half, (first + step) % 4, self.y, second)
            else:
                target = self.place(half, first, self.y, (second + step) % 4)
            self.send(half, block, target)

    def start(self):
        for half in (0, 1):
            first, second = self.coordinates(half)
            self.send(half, None, self.place(half, first, 1 - self.y, second))
        for half in (0, 1):
            self.around(half, None, 0)
        for half in (0, 1):
            self.around(half, None, 1)

    def run(self):
        for half in (0, 1):
            first, second = self.coordinates(half)
            block = self.place(half, first, 1 - self.y, second)
            self.arrive(half, block)
            self.around(half, block, 0)
            self.around(half, block, 1)
        for y in (0, 1):
            for step in (1, 3):
                for half in (0, 1):
                    first, second = self.coordinates(half)
                    block = self.place(half, (first + step) % 4, y, second)
                    self.arrive(half, block)
                    if (step == 3) == (y == 0):
                        opposite = (first + 4 - step) % 4
                        self.send(half, block, self.place(half, opposite, self.y, second))
                    self.around(half, block, 1)
        for y in (0, 1):
            for half in (0, 1):
                first, second = self.coordinates(half)
                block = self.place(half, (first + 2) % 4, y, second)
                self.arrive(half, block)
                self.around(half, block, 1)
        for hop in (0, 1, 3, 2):
            for y in (0, 1):
                for step in (1, 3):
                    for half in (0, 1):
                        first, second = self.coordinates(half)
                        block = self.place(half, (first + hop) % 4, y, (second + step) % 4)
                        self.arrive(half, block)
                        if (step == 3) == (y == 0):
                            opposite = (second + 4 - step) % 4
                            self.send(half, block, self.place(half, first, self.y, opposite))
        for hop in (0, 1, 3, 2):
            for y in (0, 1):
                for half in (0, 1):
                    first, second = self.coordinates(half)
                    self.arrive(half, self.place(half, (first + hop) % 4, y, (second + 2) % 4))

    def finish(self):
        for copy in self.started:
            copy.wait_send()


SENDS = 62


def greet(peers):
    barrier = pltpu.get_barrier_semaphore()
    for count, peer in peers:

        def one(i, carry, peer=peer):
            wide, narrow = peer(i)
            pl.semaphore_signal(barrier, inc=1, device_id=(wide, narrow), device_id_type=MESH)
            return carry

        lax.fori_loop(0, count, one, 0)
    pl.semaphore_wait(barrier, sum(count for count, _ in peers))


def attention_kernel(
    hidden,
    gain,
    query_weight,
    key_weight,
    value_weight,
    out_weight,
    cache_key,
    cache_value,
    residual,
    gathered,
    mixed,
    normed,
    joined,
    columns,
    out_columns,
    out_joined,
    kv,
    queries,
    attended,
    own_hidden,
    spread_send,
    spread_recv,
    spread_send2,
    spread_recv2,
    local_sem,
    column_send,
    column_recv,
    pair_sem,
    kv_send,
    kv_recv,
):
    me = lax.axis_index("wide")
    n = lax.axis_index("narrow")
    core = n % 2
    partner = n + 1 - 2 * core
    parity = me % 2
    group = me // KV_SHARE
    mate = me + 1 - 2 * parity

    greet(
        [
            (WIDE - 1, lambda i: ((me + 1 + i) % WIDE, n)),
            (NARROW - 1, lambda i: (me, (n + 1 + i) % NARROW)),
            (NARROW - 1, lambda i: (mate, (n + 1 + i) % NARROW)),
        ]
    )

    spread = Spread(hidden, gathered, me, n, spread_send, spread_recv)
    spread.start()
    locals_ = [
        pltpu.make_async_copy(hidden, gathered.at[me], local_sem.at[0]),
        pltpu.make_async_copy(query_weight, joined.at[:, pl.ds(0, LANE)], local_sem.at[1]),
        pltpu.make_async_copy(cache_key.at[group], kv.at[0, 0], local_sem.at[2]),
        pltpu.make_async_copy(cache_value.at[group], kv.at[1, 0], local_sem.at[3]),
        pltpu.make_async_copy(hidden, own_hidden, local_sem.at[4]),
    ]
    for copy in locals_:
        copy.start()

    half_rows = pl.ds(core * (LANE // 2), LANE // 2)

    def send_column(i, carry):
        target = (me + 1 + i) % WIDE
        cut = pl.ds(pl.multiple_of((target // KV_SHARE) * LANE, LANE), LANE)

        @pl.when(target % 2 == 0)
        def _():
            remote(
                key_weight.at[half_rows, cut], columns.at[core, me], column_send.at[0], column_recv.at[0], target, n
            ).start()

        @pl.when(target % 2 == 1)
        def _():
            remote(
                value_weight.at[half_rows, cut], columns.at[core, me], column_send.at[0], column_recv.at[0], target, n
            ).start()

        return carry

    lax.fori_loop(0, WIDE - 1, send_column, 0)
    own_cut = pl.ds(pl.multiple_of(group * LANE, LANE), LANE)

    @pl.when(parity == 0)
    def _():
        pltpu.make_async_copy(key_weight.at[half_rows, own_cut], columns.at[core, me], local_sem.at[5]).start()

    @pl.when(parity == 1)
    def _():
        pltpu.make_async_copy(value_weight.at[half_rows, own_cut], columns.at[core, me], local_sem.at[5]).start()

    spread.run()

    wait_bytes(columns.at[core, me], local_sem.at[5])
    wait_bytes(columns.at[0, pl.ds(0, WIDE - 1)], column_recv.at[0])
    swap = remote(columns.at[core], columns.at[core], pair_sem.at[0], pair_sem.at[1], me, partner)
    swap.start()

    def send_out_column(i, carry):
        target = (me + 1 + i) % WIDE
        cut = pl.ds(pl.multiple_of(target * LANE, LANE), LANE)
        remote(
            out_weight.at[half_rows, cut], out_columns.at[core, me], column_send.at[1], column_recv.at[1], target, n
        ).start()
        return carry

    lax.fori_loop(0, WIDE - 1, send_out_column, 0)
    own_out = pltpu.make_async_copy(
        out_weight.at[half_rows, pl.ds(pl.multiple_of(me * LANE, LANE), LANE)], out_columns.at[core, me], local_sem.at[6]
    )
    own_out.start()

    for copy in locals_:
        copy.wait()

    swap.wait()
    for half in (0, 1):
        for w in range(WIDE):
            joined[w * LANE + half * (LANE // 2) : w * LANE + (half + 1) * (LANE // 2), LANE:] = columns[half, w]

    def project(tile, carry):
        rows = pl.ds(pl.multiple_of(tile * LANE, LANE), LANE)
        total = jnp.zeros((LANE, LANE), F32)
        for w in range(WIDE):
            total += gathered[w, rows].astype(F32)
        average = jnp.sum(total, axis=1, keepdims=True) * (1.0 / D)
        total = jnp.zeros((LANE, LANE), F32)
        for w in range(WIDE):
            centered = gathered[w, rows].astype(F32) - average
            total += centered * centered
        scale = lax.rsqrt(jnp.sum(total, axis=1, keepdims=True) * (1.0 / D) + EPS)
        for w in range(WIDE):
            centered = gathered[w, rows].astype(F32) - average
            normed[:, w * LANE : (w + 1) * LANE] = (centered * scale * gain[w : w + 1, :]).astype(BF16)
        product = dot(normed[...], joined[...]).astype(BF16)
        queries[rows] = product[:, :LANE]
        kv[parity, n + 1, rows] = product[:, LANE:]
        return carry

    lax.fori_loop(0, ROWS // LANE, project, 0)

    for other in range(NARROW):

        @pl.when(other > n)
        def _():
            block = kv.at[parity, n + 1]
            remote(block, block, kv_send.at[0, other], kv_recv.at[parity, n], me, other).start()

        @pl.when(other >= n)
        def _():
            block = kv.at[parity, n + 1]
            remote(block, block, kv_send.at[1, other], kv_recv.at[parity, n], mate, other).start()

    for other in range(NARROW):

        @pl.when(other < n)
        def _():
            wait_bytes(kv.at[parity, other + 1], kv_recv.at[parity, other])

        @pl.when(other <= n)
        def _():
            wait_bytes(kv.at[1 - parity, other + 1], kv_recv.at[1 - parity, other])

    tile_rows = HALF

    def attend(tile, carry):
        rows = pl.ds(pl.multiple_of(tile * tile_rows, tile_rows), tile_rows)
        q = queries[rows]
        row_ids = tile * tile_rows + lax.broadcasted_iota(jnp.int32, (tile_rows, ROWS), 0)
        key_ids = lax.broadcasted_iota(jnp.int32, (tile_rows, ROWS), 1)
        causal = key_ids <= row_ids

        def block(j, state):
            highest, total, acc = state
            scores = (
                lax.dot_general(q, kv[0, j], (((1,), (1,)), ((), ())), preferred_element_type=F32) * SCALE
            )
            scores = jnp.where(jnp.logical_or(causal, j <= n), scores, -1e30)
            new = jnp.maximum(highest, jnp.max(scores, axis=1, keepdims=True))
            weights = jnp.exp(scores - new)
            fade = jnp.exp(highest - new)
            total = total * fade + jnp.sum(weights, axis=1, keepdims=True)
            acc = acc * fade + dot(weights.astype(BF16), kv[1, j])
            return new, total, acc

        start = (
            jnp.full((tile_rows, 1), -1e30, F32),
            jnp.zeros((tile_rows, 1), F32),
            jnp.zeros((tile_rows, LANE), F32),
        )
        _, total, acc = lax.fori_loop(0, n + 2, block, start)
        attended[rows] = (acc / total).astype(BF16)
        return carry

    lax.fori_loop(0, ROWS // tile_rows, attend, 0)

    spread2 = Spread(attended, mixed, me, n, spread_send2, spread_recv2)
    spread2.start()
    own_mixed = pltpu.make_async_copy(attended, mixed.at[me], local_sem.at[7])
    own_mixed.start()
    own_out.wait()
    wait_bytes(out_columns.at[0, pl.ds(0, WIDE - 1)], column_recv.at[1])
    swap_out = remote(out_columns.at[core], out_columns.at[core], pair_sem.at[2], pair_sem.at[3], me, partner)
    swap_out.start()
    spread2.run()
    swap_out.wait()
    for half in (0, 1):
        for w in range(WIDE):
            out_joined[w * LANE + half * (LANE // 2) : w * LANE + (half + 1) * (LANE // 2), :] = out_columns[half, w]
    own_mixed.wait()

    def mix(tile, carry):
        rows = pl.ds(pl.multiple_of(tile * LANE, LANE), LANE)
        total = own_hidden[rows].astype(F32)
        product = jnp.zeros((LANE, LANE), F32)
        for w in range(0, WIDE, 2):
            pair = jnp.concatenate([mixed[w, rows], mixed[w + 1, rows]], axis=1)
            product += dot(pair, out_joined[w * LANE : (w + 2) * LANE, :])
        residual[rows] = (total + product).astype(BF16)
        return carry

    lax.fori_loop(0, ROWS // LANE, mix, 0)

    spread.finish()
    spread2.finish()
    for which in range(2):
        wait_bytes(columns.at[0, pl.ds(0, WIDE - 1)], column_send.at[which])
    for other in range(NARROW):

        @pl.when(other > n)
        def _():
            wait_bytes(kv.at[parity, n + 1], kv_send.at[0, other])

        @pl.when(other >= n)
        def _():
            wait_bytes(kv.at[parity, n + 1], kv_send.at[1, other])


GROUPS = ROWS // LANE
GROUP_SLOTS = LANE // BLOCK * CAP
COLS = 512
STEPS = D // COLS


def expert_kernel(
    residual,
    gain,
    router,
    ids,
    gate_weight,
    up_weight,
    down_weight,
    result,
    gate,
    up,
    down,
    stats,
    stats_in,
    diffs,
    diffs_in,
    normed,
    outgoing,
    arrived,
    tokens,
    active,
    partial_out,
    partial_in,
    returning,
    returned,
    weight_sem,
    small_send,
    small_recv,
    local_sem,
    out_send,
    out_recv,
    pair_send,
    pair_recv,
    partial_send,
    partial_recv,
    back_send,
    back_recv,
):
    me = lax.axis_index("wide")
    n = lax.axis_index("narrow")
    core = n % 2
    high = n // 2
    partner = n + 1 - 2 * core
    far = n + 2 - 4 * high

    loads = [
        pltpu.make_async_copy(gate_weight.at[0], gate, weight_sem.at[0]),
        pltpu.make_async_copy(up_weight.at[0], up, weight_sem.at[1]),
        pltpu.make_async_copy(down_weight.at[0], down, weight_sem.at[2]),
    ]
    for load in loads:
        load.start()

    greet(
        [
            (WIDE - 1, lambda i: ((me + 1 + i) % WIDE, n)),
            (WIDE, lambda i: ((me + i) % WIDE, far)),
            (1, lambda i: (me, partner)),
        ]
    )

    eye = (
        lax.broadcasted_iota(jnp.int32, (LANE, LANE), 0) == lax.broadcasted_iota(jnp.int32, (LANE, LANE), 1)
    ).astype(F32)

    def to_row(column):
        return jnp.sum(column * eye, axis=0, keepdims=True)

    def to_column(row):
        return jnp.sum(row * eye, axis=1, keepdims=True)

    def share(mine, everyone, which):
        def one(i, carry):
            target = (me + 1 + i) % WIDE
            remote(mine, everyone.at[me], small_send.at[which], small_recv.at[which], target, n).start()
            return carry

        lax.fori_loop(0, WIDE - 1, one, 0)

    def collect(mine, everyone, which):
        everyone[me] = mine[...]
        wait_bytes(everyone.at[pl.ds(0, WIDE - 1)], small_recv.at[which])

    for g in range(GROUPS):
        values = residual[g * LANE : (g + 1) * LANE].astype(F32)
        average = jnp.sum(values, axis=1, keepdims=True) * (1.0 / LANE)
        centered = values - average
        spread_of = jnp.sum(centered * centered, axis=1, keepdims=True)
        stats[g : g + 1, :] = to_row(average)
        stats[GROUPS + g : GROUPS + g + 1, :] = to_row(spread_of)
    share(stats, stats_in, 0)

    below = lax.broadcasted_iota(jnp.int32, (LANE, LANE), 0)
    left = lax.broadcasted_iota(jnp.int32, (LANE, LANE), 1)
    earlier = jnp.logical_and(left < below, left // BLOCK == below // BLOCK).astype(BF16)
    expert_ids = lax.broadcasted_iota(jnp.int32, (LANE, EXPERTS), 1)
    slot_ids = lax.broadcasted_iota(jnp.int32, (LANE, EXPERTS * GROUP_SLOTS), 1)
    in_group = lax.broadcasted_iota(jnp.int32, (LANE, 1), 0) // BLOCK * CAP

    def chosen(g):
        pair = ids[g * LANE : (g + 1) * LANE, :]
        return [expert_ids == pair[:, k : k + 1] for k in (0, 1)]

    def placing(g):
        pair = ids[g * LANE : (g + 1) * LANE, :]
        hot = chosen(g)
        before = dot(earlier, jnp.logical_or(hot[0], hot[1]).astype(BF16))
        found = []
        for k in (0, 1):
            position = jnp.sum(jnp.where(hot[k], before, 0.0), axis=1, keepdims=True).astype(jnp.int32)
            slot = pair[:, k : k + 1] * GROUP_SLOTS + in_group + position
            found.append((slot_ids == slot).astype(BF16))
        return found

    collect(stats, stats_in, 0)
    averages = jnp.zeros((GROUPS, LANE), F32)
    for w in range(WIDE):
        averages += stats_in[w, :GROUPS]
    averages = averages * (1.0 / WIDE)
    squares = jnp.zeros((GROUPS, LANE), F32)
    for w in range(WIDE):
        shift = stats_in[w, :GROUPS] - averages
        squares += stats_in[w, GROUPS:] + LANE * (shift * shift)
    scales = lax.rsqrt(squares * (1.0 / D) + EPS)
    own_gain = gain[pl.ds(me, 1), :]
    own_router = router[me]
    for g in range(GROUPS):
        values = residual[g * LANE : (g + 1) * LANE].astype(F32)
        here = (
            (values - to_column(averages[g : g + 1])) * to_column(scales[g : g + 1]) * own_gain
        ).astype(BF16)
        first, second = placing(g)
        filled = lax.dot_general(
            first + second, here, (((0,), (0,)), ((), ())), preferred_element_type=F32
        ).astype(BF16)
        outgoing[:, g * GROUP_SLOTS : (g + 1) * GROUP_SLOTS, :] = filled.reshape(EXPERTS, GROUP_SLOTS, LANE)
        normed[g * LANE : (g + 1) * LANE] = here

    def dispatch(i, carry):
        target = (me + i) % WIDE

        @pl.when(i > 0)
        def _():
            remote(
                outgoing.at[target // 2], arrived.at[n * WIDE + me], out_send.at[0], out_recv.at[n // 2], target, n
            ).start()

        remote(
            outgoing.at[target // 2], arrived.at[n * WIDE + me], out_send.at[0], out_recv.at[n // 2], target, far
        ).start()
        return carry

    lax.fori_loop(0, WIDE, dispatch, 0)
    own_chunk = pltpu.make_async_copy(outgoing.at[me // 2], arrived.at[n * WIDE + me], local_sem.at[0])
    own_chunk.start()

    for g in range(GROUPS):
        hot = chosen(g)
        logits = dot(normed[g * LANE : (g + 1) * LANE], own_router)
        lead = jnp.sum(jnp.where(hot[0], logits, 0.0) - jnp.where(hot[1], logits, 0.0), axis=1, keepdims=True)
        diffs[g : g + 1, :] = to_row(lead)
        diffs[GROUPS + g : GROUPS + g + 1, :] = jnp.zeros((1, LANE), F32)
    share(diffs, diffs_in, 1)

    own_chunk.wait()
    wait_bytes(arrived.at[pl.ds(0, WIDE - 1)], out_recv.at[high])
    swaps = []
    for where in (high, 1 - high):
        if where is not high:
            wait_bytes(arrived.at[pl.ds(0, WIDE)], out_recv.at[where])
        part = arrived.at[pl.ds((where * 2 + core) * WIDE, WIDE)]
        swap = remote(part, part, pair_send.at[where], pair_recv.at[where], me, partner)
        swap.start()
        swaps.append(swap)
    collect(diffs, diffs_in, 1)
    for swap in swaps:
        swap.wait_send()
    for where in (0, 1):
        wait_bytes(arrived.at[pl.ds(0, WIDE)], pair_recv.at[where])
    for load in loads:
        load.wait()

    def hidden_units(which):
        for where in (0, 1):
            for w in range(WIDE):
                tokens[where * LANE : (where + 1) * LANE, w * LANE : (w + 1) * LANE] = arrived[
                    (where * 2 + which) * WIDE + w
                ]
        gated = dot(tokens[...], gate[...])
        raised = dot(tokens[...], up[...])
        active[...] = (gated / (1.0 + jnp.exp(-gated)) * raised).astype(BF16)

    hidden_units(1 - core)

    def give(step, carry):
        cut = pl.ds(pl.multiple_of(step * COLS, COLS), COLS)
        partial_out[step] = dot(active[...], down[:, cut]).astype(BF16)
        remote(
            partial_out.at[step], partial_in.at[step], partial_send.at[step], partial_recv.at[step], me, partner
        ).start()
        return carry

    lax.fori_loop(0, STEPS, give, 0)
    hidden_units(core)

    def keep(step, carry):
        cut = pl.ds(pl.multiple_of(step * COLS, COLS), COLS)
        wait_bytes(partial_in.at[step], partial_recv.at[step])
        total = (dot(active[...], down[:, cut]) + partial_in[step].astype(F32)).astype(BF16)
        for where in (0, 1):
            for k in range(COLS // LANE):
                target = step * (COLS // LANE) + k
                slot = where * WIDE + target
                returning[slot] = total[where * LANE : (where + 1) * LANE, k * LANE : (k + 1) * LANE]
                own = jnp.logical_and(target == me, where == high)

                @pl.when(jnp.logical_not(own))
                def _():
                    remote(
                        returning.at[slot],
                        returned.at[high * WIDE + me],
                        back_send.at[0],
                        back_recv.at[high],
                        target,
                        where * 2 + core,
                    ).start()

                @pl.when(own)
                def _():
                    pltpu.make_async_copy(
                        returning.at[slot], returned.at[high * WIDE + me], local_sem.at[1]
                    ).start()

        return carry

    lax.fori_loop(0, STEPS, keep, 0)

    leads = jnp.zeros((GROUPS, LANE), F32)
    for w in range(WIDE):
        leads += diffs_in[w, :GROUPS]
    heavy = 1.0 / (1.0 + jnp.exp(-leads))
    wait_bytes(returned.at[0], local_sem.at[1])
    wait_bytes(returned.at[pl.ds(0, WIDE - 1)], back_recv.at[high])
    wait_bytes(returned.at[pl.ds(0, WIDE)], back_recv.at[1 - high])
    for g in range(GROUPS):
        first, second = placing(g)
        picks = [jnp.zeros((LANE, LANE), F32)] * 2
        for where in (0, 1):
            for s in (0, 1):
                rows = jnp.concatenate(
                    [
                        returned[where * WIDE + 2 * e + s, g * GROUP_SLOTS : (g + 1) * GROUP_SLOTS, :]
                        for e in range(EXPERTS)
                    ],
                    axis=0,
                )
                picks = [picks[0] + dot(first, rows), picks[1] + dot(second, rows)]
        weight = to_column(heavy[g : g + 1])
        result[g * LANE : (g + 1) * LANE] = (
            residual[g * LANE : (g + 1) * LANE].astype(F32) + weight * picks[0] + (1.0 - weight) * picks[1]
        ).astype(BF16)

    for which in (0, 1):
        wait_bytes(stats_in.at[pl.ds(0, WIDE - 1)], small_send.at[which])
    wait_bytes(arrived.at[pl.ds(0, 2 * WIDE - 1)], out_send.at[0])
    wait_bytes(returned.at[pl.ds(0, 2 * WIDE - 1)], back_send.at[0])
    for step in range(STEPS):
        wait_bytes(partial_out.at[step], partial_send.at[step])


def body(
    hidden,
    attn_gain,
    query_weight,
    key_weight,
    value_weight,
    out_weight,
    cache_key,
    cache_value,
    mlp_gain,
    router_weight,
    expert_ids,
    gate_weight,
    up_weight,
    down_weight,
):
    anywhere = pl.BlockSpec(memory_space=pl.ANY)
    vmem = pl.BlockSpec(memory_space=pltpu.VMEM)
    dma = pltpu.SemaphoreType.DMA
    residual = pl.pallas_call(
        attention_kernel,
        out_shape=jax.ShapeDtypeStruct((ROWS, LANE), BF16),
        in_specs=[anywhere, vmem] + [anywhere] * 6,
        out_specs=vmem,
        scratch_shapes=[
            pltpu.VMEM((WIDE, ROWS, LANE), BF16),
            pltpu.VMEM((WIDE, ROWS, LANE), BF16),
            pltpu.VMEM((LANE, D), BF16),
            pltpu.VMEM((D, 2 * LANE), BF16),
            pltpu.VMEM((2, WIDE, LANE // 2, LANE), BF16),
            pltpu.VMEM((2, WIDE, LANE // 2, LANE), BF16),
            pltpu.VMEM((D, LANE), BF16),
            pltpu.VMEM((2, NARROW + 1, ROWS, LANE), BF16),
            pltpu.VMEM((ROWS, LANE), BF16),
            pltpu.VMEM((ROWS, LANE), BF16),
            pltpu.VMEM((ROWS, LANE), BF16),
            dma((SENDS,)),
            dma((2, WIDE)),
            dma((SENDS,)),
            dma((2, WIDE)),
            dma((8,)),
            dma((2,)),
            dma((2,)),
            dma((4,)),
            dma((2, NARROW)),
            dma((2, NARROW)),
        ],
        compiler_params=pltpu.CompilerParams(
            collective_id=0, has_side_effects=True, vmem_limit_bytes=56 * 2**20
        ),
    )(
        hidden,
        attn_gain.reshape(WIDE, LANE),
        query_weight,
        key_weight,
        value_weight,
        out_weight,
        cache_key,
        cache_value,
    )
    return pl.pallas_call(
        expert_kernel,
        out_shape=jax.ShapeDtypeStruct((ROWS, LANE), BF16),
        in_specs=[vmem] * 4 + [anywhere] * 3,
        out_specs=vmem,
        scratch_shapes=[
            pltpu.VMEM((D, HIDDEN), BF16),
            pltpu.VMEM((D, HIDDEN), BF16),
            pltpu.VMEM((HIDDEN, D), BF16),
            pltpu.VMEM((2 * GROUPS, LANE), F32),
            pltpu.VMEM((WIDE, 2 * GROUPS, LANE), F32),
            pltpu.VMEM((2 * GROUPS, LANE), F32),
            pltpu.VMEM((WIDE, 2 * GROUPS, LANE), F32),
            pltpu.VMEM((ROWS, LANE), BF16),
            pltpu.VMEM((EXPERTS, LANE, LANE), BF16),
            pltpu.VMEM((NARROW * WIDE, LANE, LANE), BF16),
            pltpu.VMEM((2 * LANE, D), BF16),
            pltpu.VMEM((2 * LANE, HIDDEN), BF16),
            pltpu.VMEM((STEPS, 2 * LANE, COLS), BF16),
            pltpu.VMEM((STEPS, 2 * LANE, COLS), BF16),
            pltpu.VMEM((2 * WIDE, LANE, LANE), BF16),
            pltpu.VMEM((2 * WIDE, LANE, LANE), BF16),
            dma((3,)),
            dma((2,)),
            dma((2,)),
            dma((2,)),
            dma((1,)),
            dma((2,)),
            dma((2,)),
            dma((2,)),
            dma((STEPS,)),
            dma((STEPS,)),
            dma((1,)),
            dma((2,)),
        ],
        compiler_params=pltpu.CompilerParams(
            collective_id=1, has_side_effects=True, vmem_limit_bytes=56 * 2**20
        ),
    )(
        residual,
        mlp_gain.reshape(WIDE, LANE),
        router_weight.reshape(WIDE, LANE, EXPERTS),
        expert_ids,
        gate_weight,
        up_weight,
        down_weight,
    )


def solution(mesh):
    placed = (
        P("narrow", "wide"),
        P(),
        P(None, "wide"),
        P("wide", None),
        P("wide", None),
        P("wide", None),
        P(),
        P(),
        P(),
        P(),
        P("narrow", None),
        P("wide", None, "narrow"),
        P("wide", None, "narrow"),
        P("wide", "narrow", None),
    )
    return jax.shard_map(
        body, mesh=mesh, in_specs=placed, out_specs=P("narrow", "wide"), check_vma=False
    )
```

```python
import jax
import jax.numpy as jnp
from jax import lax
from jax.experimental import pallas as pl
from jax.experimental.pallas import tpu as pltpu
from jax.sharding import PartitionSpec as P

MESH = pl.DeviceIdType.MESH
F32 = jnp.float32
BF16 = jnp.bfloat16

XN, YL, ZN = 4, 2, 4
WIDE = XN * YL * ZN
NARROW = 4
ROWS = 512
LANE = 128
D = WIDE * LANE
HALF = ROWS // 2
KV_SHARE = 4
EXPERTS = 16
CAP = 4
BLOCK = 16
HIDDEN = 800
EPS = 1e-5
SCALE = LANE**-0.5


def remote(src, dst, send_sem, recv_sem, wide, narrow):
    return pltpu.make_async_remote_copy(
        src_ref=src,
        dst_ref=dst,
        send_sem=send_sem,
        recv_sem=recv_sem,
        device_id=(wide, narrow),
        device_id_type=MESH,
    )


def wait_bytes(ref, sem):
    pltpu.make_async_copy(ref, ref, sem).wait()


def dot(a, b):
    return jnp.dot(a, b, preferred_element_type=F32)


def wide_of(x, y, z):
    return (x * YL + y) * ZN + z


def flipped(index, mask, bits):
    return sum(((index // 2**b + mask // 2**b) % 2) * 2**b for b in range(bits))


class Spread:
    def __init__(self, own, buf, me, narrow, send_sem, recv_sem):
        self.own, self.buf, self.me, self.narrow = own, buf, me, narrow
        self.send_sem, self.recv_sem = send_sem, recv_sem
        self.x = me // (YL * ZN)
        self.y = (me // ZN) % YL
        self.z = me % ZN
        self.started = []

    def place(self, half, first, y, second):
        return wide_of(first, y, second) if half == 0 else wide_of(second, y, first)

    def coordinates(self, half):
        return (self.x, self.z) if half == 0 else (self.z, self.x)

    def send(self, half, block, target):
        rows = pl.ds(half * HALF, HALF)
        own = block is None
        slot = self.me if own else block
        copy = remote(
            self.own.at[rows] if own else self.buf.at[slot, rows],
            self.buf.at[slot, rows],
            self.send_sem.at[len(self.started)],
            self.recv_sem.at[half, slot],
            target,
            self.narrow,
        )
        copy.start()
        self.started.append(copy)

    def arrive(self, half, block):
        rows = pl.ds(half * HALF, HALF)
        wait_bytes(self.buf.at[block, rows], self.recv_sem.at[half, block])

    def around(self, half, block, dimension):
        first, second = self.coordinates(half)
        for step in (1, 3):
            if dimension == 0:
                target = self.place(half, (first + step) % 4, self.y, second)
            else:
                target = self.place(half, first, self.y, (second + step) % 4)
            self.send(half, block, target)

    def start(self):
        for half in (0, 1):
            first, second = self.coordinates(half)
            self.send(half, None, self.place(half, first, 1 - self.y, second))
        for half in (0, 1):
            self.around(half, None, 0)
        for half in (0, 1):
            self.around(half, None, 1)

    def run(self):
        for half in (0, 1):
            first, second = self.coordinates(half)
            block = self.place(half, first, 1 - self.y, second)
            self.arrive(half, block)
            self.around(half, block, 0)
            self.around(half, block, 1)
        for y in (0, 1):
            for step in (1, 3):
                for half in (0, 1):
                    first, second = self.coordinates(half)
                    block = self.place(half, (first + step) % 4, y, second)
                    self.arrive(half, block)
                    if (step == 3) == (y == 0):
                        opposite = (first + 4 - step) % 4
                        self.send(half, block, self.place(half, opposite, self.y, second))
                    self.around(half, block, 1)
        for y in (0, 1):
            for half in (0, 1):
                first, second = self.coordinates(half)
                block = self.place(half, (first + 2) % 4, y, second)
                self.arrive(half, block)
                self.around(half, block, 1)
        for hop in (0, 1, 3, 2):
            for y in (0, 1):
                for step in (1, 3):
                    for half in (0, 1):
                        first, second = self.coordinates(half)
                        block = self.place(half, (first + hop) % 4, y, (second + step) % 4)
                        self.arrive(half, block)
                        if (step == 3) == (y == 0):
                            opposite = (second + 4 - step) % 4
                            self.send(half, block, self.place(half, first, self.y, opposite))
        for hop in (0, 1, 3, 2):
            for y in (0, 1):
                for half in (0, 1):
                    first, second = self.coordinates(half)
                    self.arrive(half, self.place(half, (first + hop) % 4, y, (second + 2) % 4))

    def finish(self):
        for copy in self.started:
            copy.wait_send()


SENDS = 62


def greet(peers):
    barrier = pltpu.get_barrier_semaphore()
    for count, peer in peers:

        def one(i, carry, peer=peer):
            wide, narrow = peer(i)
            pl.semaphore_signal(barrier, inc=1, device_id=(wide, narrow), device_id_type=MESH)
            return carry

        lax.fori_loop(0, count, one, 0)
    pl.semaphore_wait(barrier, sum(count for count, _ in peers))


GROUPS = ROWS // LANE
GROUP_SLOTS = LANE // BLOCK * CAP
PART = LANE // 2
COLS = 512
STEPS = D // COLS
LAG = 2
BITS = 5
ALL = NARROW * WIDE


def dot_t(a, b):
    return lax.dot_general(a, b, (((1,), (1,)), ((), ())), preferred_element_type=F32)


def layer_kernel(
    hidden,
    gain,
    query_weight,
    key_weight,
    value_weight,
    out_weight,
    cache_key,
    cache_value,
    gain_two,
    router,
    ids,
    gate_weight,
    up_weight,
    down_weight,
    result,
    gathered,
    mixed,
    normed,
    joined,
    columns,
    out_columns,
    out_joined,
    kv,
    queries,
    attended,
    own_hidden,
    residual,
    gate,
    up,
    down,
    stats,
    stats_in,
    diffs,
    diffs_in,
    placed,
    outgoing,
    arrived,
    tokens,
    active,
    partial_out,
    partial_in,
    kept,
    returning,
    returned,
    spread_send,
    spread_recv,
    spread_send2,
    spread_recv2,
    local_sem,
    column_send,
    column_recv,
    pair_sem,
    kv_send,
    kv_recv,
    weight_sem,
    small_send,
    small_recv,
    out_send,
    out_recv,
    pair_send,
    pair_recv,
    partial_send,
    partial_recv,
    back_send,
    back_recv,
):
    me = lax.axis_index("wide")
    n = lax.axis_index("narrow")
    core = n % 2
    high = n // 2
    partner = n + 1 - 2 * core
    far = n + 2 - 4 * high
    across = far + 1 - 2 * core
    parity = me % 2
    group = me // KV_SHARE
    mate = me + 1 - 2 * parity

    locals_ = [
        pltpu.make_async_copy(hidden, gathered.at[me], local_sem.at[0]),
        pltpu.make_async_copy(query_weight, joined.at[:, pl.ds(0, LANE)], local_sem.at[1]),
        pltpu.make_async_copy(cache_key.at[group], kv.at[0, 0], local_sem.at[2]),
        pltpu.make_async_copy(cache_value.at[group], kv.at[1, 0], local_sem.at[3]),
        pltpu.make_async_copy(hidden, own_hidden, local_sem.at[4]),
    ]
    for copy in locals_:
        copy.start()
    loads = [
        pltpu.make_async_copy(gate_weight.at[0], gate, weight_sem.at[0]),
        pltpu.make_async_copy(up_weight.at[0], up, weight_sem.at[1]),
        pltpu.make_async_copy(down_weight.at[0], down, weight_sem.at[2]),
    ]

    greet(
        [
            (WIDE - 1, lambda i: ((me + 1 + i) % WIDE, n)),
            (WIDE, lambda i: ((me + i) % WIDE, far)),
            (2, lambda i: (me, partner + i * (across - partner))),
            (2, lambda i: (mate, partner + i * (across - partner))),
        ]
    )

    spread = Spread(hidden, gathered, me, n, spread_send, spread_recv)
    spread.start()

    half_rows = pl.ds(core * (LANE // 2), LANE // 2)

    def send_column(i, carry):
        target = flipped(me, i + 1, BITS)
        cut = pl.ds(pl.multiple_of((target // KV_SHARE) * LANE, LANE), LANE)

        @pl.when(target % 2 == 0)
        def _():
            remote(
                key_weight.at[half_rows, cut], columns.at[core, me], column_send.at[0], column_recv.at[0], target, n
            ).start()

        @pl.when(target % 2 == 1)
        def _():
            remote(
                value_weight.at[half_rows, cut], columns.at[core, me], column_send.at[0], column_recv.at[0], target, n
            ).start()

        return carry

    lax.fori_loop(0, WIDE - 1, send_column, 0)
    own_cut = pl.ds(pl.multiple_of(group * LANE, LANE), LANE)

    @pl.when(parity == 0)
    def _():
        pltpu.make_async_copy(key_weight.at[half_rows, own_cut], columns.at[core, me], local_sem.at[5]).start()

    @pl.when(parity == 1)
    def _():
        pltpu.make_async_copy(value_weight.at[half_rows, own_cut], columns.at[core, me], local_sem.at[5]).start()

    spread.run()
    for load in loads:
        load.start()

    wait_bytes(columns.at[core, me], local_sem.at[5])
    wait_bytes(columns.at[0, pl.ds(0, WIDE - 1)], column_recv.at[0])
    swap = remote(columns.at[core], columns.at[core], pair_sem.at[0], pair_sem.at[1], me, partner)
    swap.start()

    def send_out_column(i, carry):
        target = flipped(me, i + 1, BITS)
        cut = pl.ds(pl.multiple_of(target * LANE, LANE), LANE)
        remote(
            out_weight.at[half_rows, cut], out_columns.at[core, me], column_send.at[1], column_recv.at[1], target, n
        ).start()
        return carry

    lax.fori_loop(0, WIDE - 1, send_out_column, 0)
    own_out = pltpu.make_async_copy(
        out_weight.at[half_rows, pl.ds(pl.multiple_of(me * LANE, LANE), LANE)], out_columns.at[core, me], local_sem.at[6]
    )
    own_out.start()

    for copy in locals_:
        copy.wait()

    swap.wait()
    for half in (0, 1):
        for w in range(WIDE):
            joined[w * LANE + half * (LANE // 2) : w * LANE + (half + 1) * (LANE // 2), LANE:] = columns[half, w]

    def project(tile, carry):
        rows = pl.ds(pl.multiple_of(tile * LANE, LANE), LANE)
        total = jnp.zeros((LANE, LANE), F32)
        for w in range(WIDE):
            total += gathered[w, rows].astype(F32)
        average = jnp.sum(total, axis=1, keepdims=True) * (1.0 / D)
        total = jnp.zeros((LANE, LANE), F32)
        for w in range(WIDE):
            centered = gathered[w, rows].astype(F32) - average
            total += centered * centered
        scale = lax.rsqrt(jnp.sum(total, axis=1, keepdims=True) * (1.0 / D) + EPS)
        for w in range(WIDE):
            centered = gathered[w, rows].astype(F32) - average
            normed[:, w * LANE : (w + 1) * LANE] = (centered * scale * gain[w : w + 1, :]).astype(BF16)
        product = dot(normed[...], joined[...]).astype(BF16)
        queries[rows] = product[:, :LANE]
        kv[parity, n + 1, rows] = product[:, LANE:]
        return carry

    def fresh(kind, block, half):
        return kv.at[kind, block + 1, pl.ds(half * HALF, HALF)]

    for half in (0, 1):
        lax.fori_loop(half * 2, half * 2 + 2, project, 0)
        for other in range(NARROW):

            @pl.when(other >= n)
            def _():
                block = fresh(parity, n, half)
                remote(block, block, kv_send.at[1, half, other], kv_recv.at[parity, half, n], mate, other).start()

            @pl.when(other > n)
            def _():
                block = fresh(parity, n, half)
                remote(block, block, kv_send.at[0, half, other], kv_recv.at[parity, half, n], me, other).start()

    row_ids = lax.broadcasted_iota(jnp.int32, (ROWS, ROWS), 0)
    key_ids = lax.broadcasted_iota(jnp.int32, (ROWS, ROWS), 1)
    causal = key_ids <= row_ids

    def attend(j, state):
        highest, total, acc = state
        scores = dot_t(queries[...], kv[0, j]) * SCALE
        scores = jnp.where(jnp.logical_or(causal, j <= n), scores, -1e30)
        new = jnp.maximum(highest, jnp.max(scores, axis=1, keepdims=True))
        weights = jnp.exp(scores - new)
        fade = jnp.exp(highest - new)
        total = total * fade + jnp.sum(weights, axis=1, keepdims=True)
        acc = acc * fade + dot(weights.astype(BF16), kv[1, j])
        return new, total, acc

    state = (
        jnp.full((ROWS, 1), -1e30, F32),
        jnp.zeros((ROWS, 1), F32),
        jnp.zeros((ROWS, LANE), F32),
    )
    state = lax.fori_loop(0, 1, attend, state)
    for half in (0, 1):
        for other in range(NARROW):

            @pl.when(other < n)
            def _():
                wait_bytes(fresh(parity, other, half), kv_recv.at[parity, half, other])

            @pl.when(other <= n)
            def _():
                wait_bytes(fresh(1 - parity, other, half), kv_recv.at[1 - parity, half, other])

    _, total, acc = lax.fori_loop(1, n + 2, attend, state)
    attended[...] = (acc / total).astype(BF16)

    spread2 = Spread(attended, mixed, me, n, spread_send2, spread_recv2)
    spread2.start()
    own_mixed = pltpu.make_async_copy(attended, mixed.at[me], local_sem.at[7])
    own_mixed.start()
    own_out.wait()
    wait_bytes(out_columns.at[0, pl.ds(0, WIDE - 1)], column_recv.at[1])
    swap_out = remote(out_columns.at[core], out_columns.at[core], pair_sem.at[2], pair_sem.at[3], me, partner)
    swap_out.start()

    eye = (
        lax.broadcasted_iota(jnp.int32, (LANE, LANE), 0) == lax.broadcasted_iota(jnp.int32, (LANE, LANE), 1)
    ).astype(F32)

    def to_row(column):
        return jnp.sum(column * eye, axis=0, keepdims=True)

    def to_column(row):
        return jnp.sum(row * eye, axis=1, keepdims=True)

    below = lax.broadcasted_iota(jnp.int32, (LANE, LANE), 0)
    left = lax.broadcasted_iota(jnp.int32, (LANE, LANE), 1)
    earlier = jnp.logical_and(left < below, left // BLOCK == below // BLOCK).astype(BF16)
    expert_ids = lax.broadcasted_iota(jnp.int32, (LANE, EXPERTS), 1)
    slot_ids = lax.broadcasted_iota(jnp.int32, (LANE, EXPERTS * GROUP_SLOTS), 1)
    in_group = lax.broadcasted_iota(jnp.int32, (LANE, 1), 0) // BLOCK * CAP

    def named(g):
        return [
            to_column(ids[k : k + 1, g * LANE : (g + 1) * LANE].astype(F32)).astype(jnp.int32) for k in (0, 1)
        ]

    for g in range(GROUPS):
        pair = named(g)
        hot = [expert_ids == chosen for chosen in pair]
        before = dot(earlier, jnp.logical_or(hot[0], hot[1]).astype(BF16))
        for k in (0, 1):
            position = jnp.sum(jnp.where(hot[k], before, 0.0), axis=1, keepdims=True).astype(jnp.int32)
            slot = pair[k] * GROUP_SLOTS + in_group + position
            placed[g, k] = (slot_ids == slot).astype(BF16)

    spread2.run()
    swap_out.wait()
    for half in (0, 1):
        for w in range(WIDE):
            out_joined[w * LANE + half * (LANE // 2) : w * LANE + (half + 1) * (LANE // 2), :] = out_columns[half, w]
    own_mixed.wait()

    def dispatch(part):
        def one(i, carry):
            target = flipped(me, i, BITS)
            source = outgoing.at[part, target // 2]
            slot = arrived.at[part * ALL + n * WIDE + me]

            @pl.when(i > 0)
            def _():
                remote(source, slot, out_send.at[part], out_recv.at[part, high], target, n).start()

            remote(source, slot, out_send.at[part], out_recv.at[part, high], target, far).start()
            return carry

        lax.fori_loop(0, WIDE, one, 0)
        pltpu.make_async_copy(
            outgoing.at[part, me // 2], arrived.at[part * ALL + n * WIDE + me], local_sem.at[8 + part]
        ).start()

    def share(mine, everyone, which):
        def one(i, carry):
            target = flipped(me, i + 1, BITS)
            remote(mine, everyone.at[me], small_send.at[which], small_recv.at[which], target, n).start()
            return carry

        lax.fori_loop(0, WIDE - 1, one, 0)

    def collect(mine, everyone, which):
        everyone[me] = mine[...]
        wait_bytes(everyone.at[pl.ds(0, WIDE - 1)], small_recv.at[which])

    for part in (0, 1):
        for g in (2 * part, 2 * part + 1):
            rows = slice(g * LANE, (g + 1) * LANE)
            product = jnp.zeros((LANE, LANE), F32)
            for w in range(0, WIDE, 2):
                pair = jnp.concatenate([mixed[w, rows], mixed[w + 1, rows]], axis=1)
                product += dot(pair, out_joined[w * LANE : (w + 2) * LANE, :])
            here = (own_hidden[rows].astype(F32) + product).astype(BF16)
            residual[rows] = here
            filled = lax.dot_general(
                placed[g, 0] + placed[g, 1], here, (((0,), (0,)), ((), ())), preferred_element_type=F32
            ).astype(BF16)
            at = (g % 2) * GROUP_SLOTS
            outgoing[part, :, at : at + GROUP_SLOTS, :] = filled.reshape(EXPERTS, GROUP_SLOTS, LANE)
        dispatch(part)

    for g in range(GROUPS):
        values = residual[g * LANE : (g + 1) * LANE].astype(F32)
        average = jnp.sum(values, axis=1, keepdims=True) * (1.0 / LANE)
        centered = values - average
        deviations = jnp.sum(centered * centered, axis=1, keepdims=True)
        stats[g : g + 1, :] = to_row(average)
        stats[GROUPS + g : GROUPS + g + 1, :] = to_row(deviations)
    share(stats, stats_in, 0)

    def norm_tokens(part, source):
        base = part * ALL + source * WIDE
        total = jnp.zeros((PART, LANE), F32)
        for w in range(WIDE):
            total += arrived[base + w].astype(F32)
        average = jnp.sum(total, axis=1, keepdims=True) * (1.0 / D)
        total = jnp.zeros((PART, LANE), F32)
        for w in range(WIDE):
            centered = arrived[base + w].astype(F32) - average
            total += centered * centered
        scale = lax.rsqrt(jnp.sum(total, axis=1, keepdims=True) * (1.0 / D) + EPS)
        where = pl.ds(pl.multiple_of((source % 2) * LANE + (source // 2) * PART, PART), PART)
        for w in range(WIDE):
            centered = arrived[base + w].astype(F32) - average
            tokens[where, w * LANE : (w + 1) * LANE] = (centered * scale * gain_two[w : w + 1, :]).astype(BF16)

    def receive(part):
        wait_bytes(outgoing.at[part, 0], local_sem.at[8 + part])
        swaps = []
        for order, where in enumerate((high, 1 - high)):
            count = WIDE - 1 if order == 0 else WIDE
            wait_bytes(arrived.at[pl.ds(0, count)], out_recv.at[part, where])
            piece = arrived.at[pl.ds(part * ALL + (where * 2 + core) * WIDE, WIDE)]
            swap = remote(piece, piece, pair_send.at[part, where], pair_recv.at[part, where], me, partner)
            swap.start()
            swaps.append(swap)
        return swaps

    def experts(part):
        for where in (0, 1):
            norm_tokens(part, where * 2 + core)
        for where in (0, 1):
            wait_bytes(arrived.at[pl.ds(0, WIDE)], pair_recv.at[part, where])
            norm_tokens(part, where * 2 + 1 - core)
        gated = dot_t(tokens[...], gate[...])
        raised = dot_t(tokens[...], up[...])
        active[...] = (gated / (1.0 + jnp.exp(-gated)) * raised).astype(BF16)

        def step(k, carry):
            @pl.when(k < STEPS)
            def _():
                block = flipped(me // 4, k, 3)
                cut = pl.ds(pl.multiple_of(block * COLS, COLS), COLS)
                total = dot(active[...], down[:, cut])

                @pl.when(core == 0)
                def _():
                    kept[k] = total[:LANE]
                    partial_out[part * STEPS + k] = total[LANE:].astype(BF16)

                @pl.when(core == 1)
                def _():
                    kept[k] = total[LANE:]
                    partial_out[part * STEPS + k] = total[:LANE].astype(BF16)

                at = part * STEPS + k
                remote(
                    partial_out.at[at], partial_in.at[at], partial_send.at[at], partial_recv.at[at], me, partner
                ).start()

            @pl.when(k >= LAG)
            def _():
                late = k - LAG
                block = flipped(me // 4, late, 3)
                at = part * STEPS + late
                wait_bytes(partial_in.at[at], partial_recv.at[at])
                total = (kept[late] + partial_in[at].astype(F32)).astype(BF16)
                base = part * 2 * WIDE + block * 4
                for where in (0, 1):
                    for q in range(4):
                        returning[base + where * WIDE + q] = total[
                            where * PART : (where + 1) * PART, q * LANE : (q + 1) * LANE
                        ]
                for q in range(4):
                    spot = flipped(me % 4, q, 2)
                    target = block * 4 + spot
                    for turn in (0, 1):
                        where = high if turn == 0 else 1 - high
                        slot = returning.at[base + where * WIDE + spot]
                        home = returned.at[part * 2 * WIDE + high * WIDE + me]
                        sems = back_send.at[part], back_recv.at[part, high]
                        if turn == 1 or q > 0:
                            remote(slot, home, *sems, target, where * 2 + core).start()
                        else:

                            @pl.when(late > 0)
                            def _():
                                remote(slot, home, *sems, target, where * 2 + core).start()

                            @pl.when(late == 0)
                            def _():
                                pltpu.make_async_copy(slot, home, local_sem.at[10 + part]).start()

            return carry

        lax.fori_loop(0, STEPS + LAG, step, 0)

    def combine(part):
        wait_bytes(returned.at[0], local_sem.at[10 + part])
        wait_bytes(returned.at[pl.ds(0, WIDE - 1)], back_recv.at[part, high])
        wait_bytes(returned.at[pl.ds(0, WIDE)], back_recv.at[part, 1 - high])
        for g in (2 * part, 2 * part + 1):
            at = (g % 2) * GROUP_SLOTS
            picks = [jnp.zeros((LANE, LANE), F32)] * 2
            for where in (0, 1):
                for s in (0, 1):
                    rows = jnp.concatenate(
                        [
                            returned[(part * 2 + where) * WIDE + 2 * e + s, at : at + GROUP_SLOTS, :]
                            for e in range(EXPERTS)
                        ],
                        axis=0,
                    )
                    picks = [picks[k] + dot(placed[g, k], rows) for k in (0, 1)]
            weight = to_column(heavy[g : g + 1])
            result[g * LANE : (g + 1) * LANE] = (
                residual[g * LANE : (g + 1) * LANE].astype(F32) + weight * picks[0] + (1.0 - weight) * picks[1]
            ).astype(BF16)

    swaps = receive(0)

    collect(stats, stats_in, 0)
    averages = jnp.zeros((GROUPS, LANE), F32)
    for w in range(WIDE):
        averages += stats_in[w, :GROUPS]
    averages = averages * (1.0 / WIDE)
    squares = jnp.zeros((GROUPS, LANE), F32)
    for w in range(WIDE):
        shift = stats_in[w, :GROUPS] - averages
        squares += stats_in[w, GROUPS:] + LANE * (shift * shift)
    scales = lax.rsqrt(squares * (1.0 / D) + EPS)
    own_gain = gain_two[pl.ds(me, 1), :]
    own_router = router[:, pl.ds(pl.multiple_of(me * LANE, LANE), LANE)]
    for g in range(GROUPS):
        values = residual[g * LANE : (g + 1) * LANE].astype(F32)
        here = ((values - to_column(averages[g : g + 1])) * to_column(scales[g : g + 1]) * own_gain).astype(BF16)
        logits = dot_t(here, own_router)
        pair = named(g)
        lead = jnp.sum(
            jnp.where(expert_ids == pair[0], logits, 0.0) - jnp.where(expert_ids == pair[1], logits, 0.0),
            axis=1,
            keepdims=True,
        )
        diffs[g : g + 1, :] = to_row(lead)
        diffs[GROUPS + g : GROUPS + g + 1, :] = jnp.zeros((1, LANE), F32)
    share(diffs, diffs_in, 1)

    for load in loads:
        load.wait()
    experts(0)
    swaps += receive(1)
    experts(1)

    collect(diffs, diffs_in, 1)
    leads = jnp.zeros((GROUPS, LANE), F32)
    for w in range(WIDE):
        leads += diffs_in[w, :GROUPS]
    heavy = 1.0 / (1.0 + jnp.exp(-leads))
    combine(0)
    combine(1)

    spread.finish()
    spread2.finish()
    for swap in swaps:
        swap.wait_send()
    for which in range(2):
        wait_bytes(columns.at[0, pl.ds(0, WIDE - 1)], column_send.at[which])
        wait_bytes(stats_in.at[pl.ds(0, WIDE - 1)], small_send.at[which])
        wait_bytes(arrived.at[pl.ds(0, 2 * WIDE - 1)], out_send.at[which])
        wait_bytes(returned.at[pl.ds(0, 2 * WIDE - 1)], back_send.at[which])
    for half in (0, 1):
        for other in range(NARROW):

            @pl.when(other > n)
            def _():
                wait_bytes(fresh(parity, n, half), kv_send.at[0, half, other])

            @pl.when(other >= n)
            def _():
                wait_bytes(fresh(parity, n, half), kv_send.at[1, half, other])

    for at in range(2 * STEPS):
        wait_bytes(partial_out.at[at], partial_send.at[at])


def body(
    hidden,
    attn_gain,
    query_weight,
    key_weight,
    value_weight,
    out_weight,
    cache_key,
    cache_value,
    mlp_gain,
    router_weight,
    expert_ids,
    gate_weight,
    up_weight,
    down_weight,
):
    anywhere = pl.BlockSpec(memory_space=pl.ANY)
    vmem = pl.BlockSpec(memory_space=pltpu.VMEM)
    dma = pltpu.SemaphoreType.DMA

    def held(*shape, kind=BF16):
        return pltpu.VMEM(shape, kind)

    return pl.pallas_call(
        layer_kernel,
        out_shape=jax.ShapeDtypeStruct((ROWS, LANE), BF16),
        in_specs=[anywhere, vmem] + [anywhere] * 6 + [vmem] * 3 + [anywhere] * 3,
        out_specs=vmem,
        scratch_shapes=[
            held(WIDE, ROWS, LANE),
            held(WIDE, ROWS, LANE),
            held(LANE, D),
            held(D, 2 * LANE),
            held(2, WIDE, LANE // 2, LANE),
            held(2, WIDE, LANE // 2, LANE),
            held(D, LANE),
            held(2, NARROW + 1, ROWS, LANE),
            held(ROWS, LANE),
            held(ROWS, LANE),
            held(ROWS, LANE),
            held(ROWS, LANE),
            held(HIDDEN, D),
            held(HIDDEN, D),
            held(HIDDEN, D),
            held(2 * GROUPS, LANE, kind=F32),
            held(WIDE, 2 * GROUPS, LANE, kind=F32),
            held(2 * GROUPS, LANE, kind=F32),
            held(WIDE, 2 * GROUPS, LANE, kind=F32),
            held(GROUPS, 2, LANE, EXPERTS * GROUP_SLOTS),
            held(2, EXPERTS, PART, LANE),
            held(2 * ALL, PART, LANE),
            held(2 * LANE, D),
            held(2 * LANE, HIDDEN),
            held(2 * STEPS, LANE, COLS),
            held(2 * STEPS, LANE, COLS),
            held(STEPS, LANE, COLS, kind=F32),
            held(4 * WIDE, PART, LANE),
            held(4 * WIDE, PART, LANE),
            dma((SENDS,)),
            dma((2, WIDE)),
            dma((SENDS,)),
            dma((2, WIDE)),
            dma((12,)),
            dma((2,)),
            dma((2,)),
            dma((4,)),
            dma((2, 2, NARROW)),
            dma((2, 2, NARROW)),
            dma((3,)),
            dma((2,)),
            dma((2,)),
            dma((2,)),
            dma((2, 2)),
            dma((2, 2)),
            dma((2, 2)),
            dma((2 * STEPS,)),
            dma((2 * STEPS,)),
            dma((2,)),
            dma((2, 2)),
        ],
        compiler_params=pltpu.CompilerParams(
            collective_id=0, has_side_effects=True, vmem_limit_bytes=60 * 2**20
        ),
    )(
        hidden,
        attn_gain.reshape(WIDE, LANE),
        query_weight,
        key_weight,
        value_weight,
        out_weight,
        cache_key,
        cache_value,
        mlp_gain.reshape(WIDE, LANE),
        router_weight.T,
        expert_ids.T,
        gate_weight.swapaxes(1, 2),
        up_weight.swapaxes(1, 2),
        down_weight,
    )


def solution(mesh):
    placed = (
        P("narrow", "wide"),
        P(),
        P(None, "wide"),
        P("wide", None),
        P("wide", None),
        P("wide", None),
        P(),
        P(),
        P(),
        P(),
        P("narrow", None),
        P("wide", None, "narrow"),
        P("wide", None, "narrow"),
        P("wide", "narrow", None),
    )
    return jax.shard_map(
        body, mesh=mesh, in_specs=placed, out_specs=P("narrow", "wide"), check_vma=False
    )
```

```python
import jax
import jax.numpy as jnp
from jax import lax
from jax.experimental import pallas as pl
from jax.experimental.pallas import tpu as pltpu
from jax.sharding import PartitionSpec as P

MESH = pl.DeviceIdType.MESH
F32 = jnp.float32
BF16 = jnp.bfloat16

XN, YL, ZN = 4, 2, 4
WIDE = XN * YL * ZN
NARROW = 4
ROWS = 512
LANE = 128
D = WIDE * LANE
HALF = ROWS // 2
KV_SHARE = 4
EXPERTS = 16
CAP = 4
BLOCK = 16
HIDDEN = 800
EPS = 1e-5
SCALE = LANE**-0.5


def remote(src, dst, send_sem, recv_sem, wide, narrow):
    return pltpu.make_async_remote_copy(
        src_ref=src,
        dst_ref=dst,
        send_sem=send_sem,
        recv_sem=recv_sem,
        device_id=(wide, narrow),
        device_id_type=MESH,
    )


def wait_bytes(ref, sem):
    pltpu.make_async_copy(ref, ref, sem).wait()


def dot(a, b):
    return jnp.dot(a, b, preferred_element_type=F32)


def wide_of(x, y, z):
    return (x * YL + y) * ZN + z


def flipped(index, mask, bits):
    return sum(((index // 2**b + mask // 2**b) % 2) * 2**b for b in range(bits))


class Spread:
    def __init__(self, own, buf, me, narrow, send_sem, recv_sem, begin, visit):
        self.own, self.buf, self.me, self.narrow = own, buf, me, narrow
        self.begin, self.visit = begin, visit
        self.send_sem, self.recv_sem = send_sem, recv_sem
        self.x = me // (YL * ZN)
        self.y = (me // ZN) % YL
        self.z = me % ZN
        self.started = []

    def place(self, half, first, y, second):
        return wide_of(first, y, second) if half == 0 else wide_of(second, y, first)

    def coordinates(self, half):
        return (self.x, self.z) if half == 0 else (self.z, self.x)

    def send(self, half, block, target):
        rows = pl.ds(half * HALF, HALF)
        own = block is None
        slot = self.me if own else block
        copy = remote(
            self.own.at[rows] if own else self.buf.at[slot, rows],
            self.buf.at[slot, rows],
            self.send_sem.at[len(self.started)],
            self.recv_sem.at[half, slot],
            target,
            self.narrow,
        )
        copy.start()
        self.started.append(copy)

    def arrive(self, half, block):
        rows = pl.ds(half * HALF, HALF)
        wait_bytes(self.buf.at[block, rows], self.recv_sem.at[half, block])

    def around(self, half, block, dimension):
        first, second = self.coordinates(half)
        for step in (1, 3):
            if dimension == 0:
                target = self.place(half, (first + step) % 4, self.y, second)
            else:
                target = self.place(half, first, self.y, (second + step) % 4)
            self.send(half, block, target)

    def start(self):
        for half in (0, 1):
            first, second = self.coordinates(half)
            self.send(half, None, self.place(half, first, 1 - self.y, second))
        for half in (0, 1):
            self.around(half, None, 0)
        for half in (0, 1):
            self.around(half, None, 1)

    def run(self):
        for half in (0, 1):
            first, second = self.coordinates(half)
            block = self.place(half, first, 1 - self.y, second)
            self.arrive(half, block)
            self.around(half, block, 0)
            self.around(half, block, 1)
        self.begin()
        for half in (0, 1):
            first, second = self.coordinates(half)
            self.visit(self.place(half, first, 1 - self.y, second), half)
        for y in (0, 1):
            for step in (1, 3):
                for half in (0, 1):
                    first, second = self.coordinates(half)
                    block = self.place(half, (first + step) % 4, y, second)
                    self.arrive(half, block)
                    if (step == 3) == (y == 0):
                        opposite = (first + 4 - step) % 4
                        self.send(half, block, self.place(half, opposite, self.y, second))
                    self.around(half, block, 1)
                    self.visit(block, half)
        for y in (0, 1):
            for half in (0, 1):
                first, second = self.coordinates(half)
                block = self.place(half, (first + 2) % 4, y, second)
                self.arrive(half, block)
                self.around(half, block, 1)
                self.visit(block, half)
        for hop in (0, 1, 3, 2):
            for y in (0, 1):
                for step in (1, 3):
                    for half in (0, 1):
                        first, second = self.coordinates(half)
                        block = self.place(half, (first + hop) % 4, y, (second + step) % 4)
                        self.arrive(half, block)
                        if (step == 3) == (y == 0):
                            opposite = (second + 4 - step) % 4
                            self.send(half, block, self.place(half, first, self.y, opposite))
                        self.visit(block, half)
        for hop in (0, 1, 3, 2):
            for y in (0, 1):
                for half in (0, 1):
                    first, second = self.coordinates(half)
                    block = self.place(half, (first + hop) % 4, y, (second + 2) % 4)
                    self.arrive(half, block)
                    self.visit(block, half)

    def finish(self):
        for copy in self.started:
            copy.wait_send()


SENDS = 62


def greet(peers):
    barrier = pltpu.get_barrier_semaphore()
    for count, peer in peers:

        def one(i, carry, peer=peer):
            wide, narrow = peer(i)
            pl.semaphore_signal(barrier, inc=1, device_id=(wide, narrow), device_id_type=MESH)
            return carry

        lax.fori_loop(0, count, one, 0)
    pl.semaphore_wait(barrier, sum(count for count, _ in peers))


GROUPS = ROWS // LANE
GROUP_SLOTS = LANE // BLOCK * CAP
PARTS = ((0, 2), (2, 1), (3, 1))
OWN = 2 * GROUP_SLOTS
COLS = 512
STEPS = D // COLS
LAG = 2
BITS = 5
ALL = NARROW * WIDE


def dot_t(a, b):
    return lax.dot_general(a, b, (((1,), (1,)), ((), ())), preferred_element_type=F32)


def layer_kernel(
    hidden,
    gain,
    query_weight,
    key_weight,
    value_weight,
    out_weight,
    cache_key,
    cache_value,
    gain_two,
    router,
    ids,
    gate_weight,
    up_weight,
    down_weight,
    result,
    gathered,
    mixed,
    normed,
    joined,
    columns,
    out_columns,
    out_joined,
    kv,
    queries,
    attended,
    own_hidden,
    residual,
    shift,
    sums,
    mixture,
    gate,
    up,
    down,
    stats,
    stats_in,
    diffs,
    diffs_in,
    placed,
    outgoing,
    arrived,
    tokens,
    active,
    partial_out,
    partial_in,
    kept,
    returning,
    returned,
    spread_send,
    spread_recv,
    spread_send2,
    spread_recv2,
    local_sem,
    column_send,
    column_recv,
    pair_sem,
    kv_send,
    kv_recv,
    weight_sem,
    small_send,
    small_recv,
    out_send,
    out_recv,
    pair_send,
    pair_recv,
    partial_send,
    partial_recv,
    back_send,
    back_recv,
):
    me = lax.axis_index("wide")
    n = lax.axis_index("narrow")
    core = n % 2
    high = n // 2
    partner = n + 1 - 2 * core
    far = n + 2 - 4 * high
    across = far + 1 - 2 * core
    parity = me % 2
    group = me // KV_SHARE
    mate = me + 1 - 2 * parity

    locals_ = [
        pltpu.make_async_copy(hidden, gathered.at[me], local_sem.at[0]),
        pltpu.make_async_copy(query_weight, joined.at[:, pl.ds(0, LANE)], local_sem.at[1]),
        pltpu.make_async_copy(cache_key.at[group], kv.at[0, 0], local_sem.at[2]),
        pltpu.make_async_copy(cache_value.at[group], kv.at[1, 0], local_sem.at[3]),
        pltpu.make_async_copy(hidden, own_hidden, local_sem.at[4]),
    ]
    for copy in locals_:
        copy.start()
    loads = [
        pltpu.make_async_copy(gate_weight.at[0], gate, weight_sem.at[0]),
        pltpu.make_async_copy(up_weight.at[0], up, weight_sem.at[1]),
        pltpu.make_async_copy(down_weight.at[0], down, weight_sem.at[2]),
    ]

    greet(
        [
            (WIDE - 1, lambda i: ((me + 1 + i) % WIDE, n)),
            (WIDE, lambda i: ((me + i) % WIDE, far)),
            (2, lambda i: (me, partner + i * (across - partner))),
            (2, lambda i: (mate, partner + i * (across - partner))),
        ]
    )

    def gather_own():
        locals_[4].wait()
        own = own_hidden[...].astype(F32)
        shift[...] = jnp.broadcast_to(jnp.sum(own, axis=1, keepdims=True) * (1.0 / LANE), (ROWS, LANE))
        own = own - shift[...]
        sums[0] = own
        sums[1] = own * own

    def gather_sums(block, half):
        rows = slice(half * HALF, (half + 1) * HALF)
        moved = gathered[block, rows].astype(F32) - shift[rows]
        sums[0, rows] += moved
        sums[1, rows] += moved * moved

    spread = Spread(hidden, gathered, me, n, spread_send, spread_recv, gather_own, gather_sums)
    spread.start()

    half_rows = pl.ds(core * (LANE // 2), LANE // 2)

    def send_column(i, carry):
        target = flipped(me, i + 1, BITS)
        cut = pl.ds(pl.multiple_of((target // KV_SHARE) * LANE, LANE), LANE)

        @pl.when(target % 2 == 0)
        def _():
            remote(
                key_weight.at[half_rows, cut], columns.at[core, me], column_send.at[0], column_recv.at[0], target, n
            ).start()

        @pl.when(target % 2 == 1)
        def _():
            remote(
                value_weight.at[half_rows, cut], columns.at[core, me], column_send.at[0], column_recv.at[0], target, n
            ).start()

        return carry

    lax.fori_loop(0, WIDE - 1, send_column, 0)
    own_cut = pl.ds(pl.multiple_of(group * LANE, LANE), LANE)

    @pl.when(parity == 0)
    def _():
        pltpu.make_async_copy(key_weight.at[half_rows, own_cut], columns.at[core, me], local_sem.at[5]).start()

    @pl.when(parity == 1)
    def _():
        pltpu.make_async_copy(value_weight.at[half_rows, own_cut], columns.at[core, me], local_sem.at[5]).start()

    spread.run()
    for load in loads:
        load.start()

    wait_bytes(columns.at[core, me], local_sem.at[5])
    wait_bytes(columns.at[0, pl.ds(0, WIDE - 1)], column_recv.at[0])
    swap = remote(columns.at[core], columns.at[core], pair_sem.at[0], pair_sem.at[1], me, partner)
    swap.start()

    def send_out_column(i, carry):
        target = flipped(me, i + 1, BITS)
        cut = pl.ds(pl.multiple_of(target * LANE, LANE), LANE)
        remote(
            out_weight.at[half_rows, cut], out_columns.at[core, me], column_send.at[1], column_recv.at[1], target, n
        ).start()
        return carry

    lax.fori_loop(0, WIDE - 1, send_out_column, 0)
    own_out = pltpu.make_async_copy(
        out_weight.at[half_rows, pl.ds(pl.multiple_of(me * LANE, LANE), LANE)], out_columns.at[core, me], local_sem.at[6]
    )
    own_out.start()

    for copy in locals_[:4]:
        copy.wait()

    swap.wait()
    for half in (0, 1):
        for w in range(WIDE):
            joined[w * LANE + half * (LANE // 2) : w * LANE + (half + 1) * (LANE // 2), LANE:] = columns[half, w]

    def project(tile, carry):
        rows = pl.ds(pl.multiple_of(tile * LANE, LANE), LANE)
        offset = jnp.sum(sums[0, rows], axis=1, keepdims=True) * (1.0 / D)
        square = jnp.sum(sums[1, rows], axis=1, keepdims=True) * (1.0 / D)
        average = jnp.max(shift[rows], axis=1, keepdims=True) + offset
        scale = lax.rsqrt(jnp.maximum(square - offset * offset, 0.0) + EPS)
        for w in range(WIDE):
            centered = gathered[w, rows].astype(F32) - average
            normed[:, w * LANE : (w + 1) * LANE] = (centered * scale * gain[w : w + 1, :]).astype(BF16)
        product = dot(normed[...], joined[...]).astype(BF16)
        queries[rows] = product[:, :LANE]
        kv[parity, n + 1, rows] = product[:, LANE:]
        return carry

    def fresh(kind, block, half):
        return kv.at[kind, block + 1, pl.ds(half * HALF, HALF)]

    def give(kind, half, block, order, wide, narrow):
        piece = fresh(kind, block, half)
        remote(piece, piece, kv_send.at[half, order], kv_recv.at[kind, half, block], wide, narrow).start()

    def take(kind, half, block):
        wait_bytes(fresh(kind, block, half), kv_recv.at[kind, half, block])

    for half in (0, 1):
        lax.fori_loop(half * 2, half * 2 + 2, project, 0)
        give(parity, half, n, 0, mate, n)

        @pl.when(high == 0)
        def _():
            give(parity, half, n, 1, me, far)
            give(parity, half, n, 2, mate, far)

        @pl.when(core == 0)
        def _():
            give(parity, half, n, 3, me, partner)

    row_ids = lax.broadcasted_iota(jnp.int32, (ROWS, ROWS), 0)
    key_ids = lax.broadcasted_iota(jnp.int32, (ROWS, ROWS), 1)
    causal = key_ids <= row_ids

    def attend(j, state):
        highest, total, acc = state
        scores = dot_t(queries[...], kv[0, j]) * SCALE
        scores = jnp.where(jnp.logical_or(causal, j <= n), scores, -1e30)
        new = jnp.maximum(highest, jnp.max(scores, axis=1, keepdims=True))
        weights = jnp.exp(scores - new)
        fade = jnp.exp(highest - new)
        total = total * fade + jnp.sum(weights, axis=1, keepdims=True)
        acc = acc * fade + dot(weights.astype(BF16), kv[1, j])
        return new, total, acc

    state = (
        jnp.full((ROWS, 1), -1e30, F32),
        jnp.zeros((ROWS, 1), F32),
        jnp.zeros((ROWS, LANE), F32),
    )
    state = lax.fori_loop(0, 1, attend, state)
    own_out.wait()
    wait_bytes(out_columns.at[0, pl.ds(0, WIDE - 1)], column_recv.at[1])
    swap_out = remote(out_columns.at[core], out_columns.at[core], pair_sem.at[2], pair_sem.at[3], me, partner)
    swap_out.start()
    for half in (0, 1):
        take(1 - parity, half, n)

        @pl.when(core == 0)
        def _():
            give(1 - parity, half, n, 4, me, partner)

        @pl.when(high == 1)
        def _():
            take(parity, half, far)
            give(parity, half, far, 5, me, partner)
            take(1 - parity, half, far)
            give(1 - parity, half, far, 6, me, partner)

    eye = (
        lax.broadcasted_iota(jnp.int32, (LANE, LANE), 0) == lax.broadcasted_iota(jnp.int32, (LANE, LANE), 1)
    ).astype(F32)

    def to_row(column):
        return jnp.sum(column * eye, axis=0, keepdims=True)

    def to_column(row):
        return jnp.sum(row * eye, axis=1, keepdims=True)

    below = lax.broadcasted_iota(jnp.int32, (LANE, LANE), 0)
    left = lax.broadcasted_iota(jnp.int32, (LANE, LANE), 1)
    earlier = jnp.logical_and(left < below, left // BLOCK == below // BLOCK).astype(BF16)
    expert_ids = lax.broadcasted_iota(jnp.int32, (LANE, EXPERTS), 1)
    slot_ids = lax.broadcasted_iota(jnp.int32, (LANE, EXPERTS * GROUP_SLOTS), 1)
    in_group = lax.broadcasted_iota(jnp.int32, (LANE, 1), 0) // BLOCK * CAP

    def named(g):
        return [
            to_column(ids[k : k + 1, g * LANE : (g + 1) * LANE].astype(F32)).astype(jnp.int32) for k in (0, 1)
        ]

    for g in range(GROUPS):
        pair = named(g)
        hot = [expert_ids == chosen for chosen in pair]
        before = dot(earlier, jnp.logical_or(hot[0], hot[1]).astype(BF16))
        for k in (0, 1):
            position = jnp.sum(jnp.where(hot[k], before, 0.0), axis=1, keepdims=True).astype(jnp.int32)
            slot = pair[k] * GROUP_SLOTS + in_group + position
            placed[g, k] = (slot_ids == slot).astype(BF16)

    swap_out.wait()
    for half in (0, 1):
        for w in range(WIDE):
            out_joined[w * LANE + half * (LANE // 2) : w * LANE + (half + 1) * (LANE // 2), :] = out_columns[half, w]

    for half in (0, 1):

        @pl.when(core == 1)
        def _():
            take(parity, half, partner)
            take(1 - parity, half, partner)

        @pl.when(high == 1)
        def _():
            take(parity, half, across)
            take(1 - parity, half, across)

    _, total, acc = lax.fori_loop(1, n + 2, attend, state)
    attended[...] = (acc / total).astype(BF16)

    def out_rows(block):
        return out_joined[pl.ds(pl.multiple_of(block * LANE, LANE), LANE), :]

    def mix_own():
        mixture[...] = own_hidden[...].astype(F32) + dot(attended[...], out_rows(me))

    def gather_products(block, half):
        rows = slice(half * HALF, (half + 1) * HALF)
        mixture[rows] += dot(mixed[block, rows], out_rows(block))

    spread2 = Spread(attended, mixed, me, n, spread_send2, spread_recv2, mix_own, gather_products)
    spread2.start()

    spread2.run()

    def dispatch(part):
        groups = pl.ds(*PARTS[part])
        slot = arrived.at[n * WIDE + me, groups]

        def one(i, carry):
            target = flipped(me, i, BITS)
            source = outgoing.at[target // 2, groups]

            @pl.when(i > 0)
            def _():
                remote(source, slot, out_send.at[part], out_recv.at[part, high], target, n).start()

            remote(source, slot, out_send.at[part], out_recv.at[part, high], target, far).start()
            return carry

        lax.fori_loop(0, WIDE, one, 0)
        pltpu.make_async_copy(outgoing.at[me // 2, groups], slot, local_sem.at[8 + part]).start()

    def share(mine, everyone, which):
        def one(i, carry):
            target = flipped(me, i + 1, BITS)
            remote(mine, everyone.at[me], small_send.at[which], small_recv.at[which], target, n).start()
            return carry

        lax.fori_loop(0, WIDE - 1, one, 0)

    def collect(mine, everyone, which):
        everyone[me] = mine[...]
        wait_bytes(everyone.at[pl.ds(0, WIDE - 1)], small_recv.at[which])

    def deviations_of(g):
        values = residual[g * LANE : (g + 1) * LANE].astype(F32)
        average = jnp.sum(values, axis=1, keepdims=True) * (1.0 / LANE)
        centered = values - average
        deviations = jnp.sum(centered * centered, axis=1, keepdims=True)
        stats[g : g + 1, :] = to_row(average)
        stats[GROUPS + g : GROUPS + g + 1, :] = to_row(deviations)

    for part, (first_group, count) in enumerate(PARTS):
        for g in range(first_group, first_group + count):
            rows = slice(g * LANE, (g + 1) * LANE)
            here = mixture[rows].astype(BF16)
            residual[rows] = here
            filled = lax.dot_general(
                placed[g, 0] + placed[g, 1], here, (((0,), (0,)), ((), ())), preferred_element_type=F32
            ).astype(BF16)
            outgoing[:, g] = filled.reshape(EXPERTS, GROUP_SLOTS, LANE)
        dispatch(part)
        if part == 0:
            for g in range(GROUPS):
                residual[g * LANE : (g + 1) * LANE] = mixture[g * LANE : (g + 1) * LANE].astype(BF16)
                deviations_of(g)
            share(stats, stats_in, 0)

    def norm_tokens(part, source):
        first_group, count = PARTS[part]
        size = count * GROUP_SLOTS

        def values(w):
            block = arrived[source * WIDE + w, first_group : first_group + count]
            return block.reshape(size, LANE).astype(F32)

        total = jnp.zeros((size, LANE), F32)
        for w in range(WIDE):
            total += values(w)
        average = jnp.sum(total, axis=1, keepdims=True) * (1.0 / D)
        total = jnp.zeros((size, LANE), F32)
        for w in range(WIDE):
            centered = values(w) - average
            total += centered * centered
        scale = lax.rsqrt(jnp.sum(total, axis=1, keepdims=True) * (1.0 / D) + EPS)
        where = pl.ds(pl.multiple_of(((source % 2) * 2 + source // 2) * size, GROUP_SLOTS), size)
        for w in range(WIDE):
            centered = values(w) - average
            tokens[where, w * LANE : (w + 1) * LANE] = (centered * scale * gain_two[w : w + 1, :]).astype(BF16)

    swaps = []

    def receive(part):
        groups = pl.ds(*PARTS[part])
        wait_bytes(outgoing.at[0, groups], local_sem.at[8 + part])
        for order, where in enumerate((high, 1 - high)):
            blocks = WIDE - 1 if order == 0 else WIDE
            wait_bytes(arrived.at[pl.ds(0, blocks), groups], out_recv.at[part, where])
            piece = arrived.at[pl.ds((where * 2 + core) * WIDE, WIDE), groups]
            swap = remote(piece, piece, pair_send.at[part, where], pair_recv.at[part, where], me, partner)
            swap.start()
            swaps.append(swap)

    def experts(part):
        first_group, count = PARTS[part]
        groups = pl.ds(first_group, count)
        size = count * GROUP_SLOTS
        rows = count * OWN
        everything = pl.ds(0, 2 * rows)
        for where in (0, 1):
            norm_tokens(part, where * 2 + core)
        for where in (0, 1):
            wait_bytes(arrived.at[pl.ds(0, WIDE), groups], pair_recv.at[part, where])
            norm_tokens(part, where * 2 + 1 - core)
        gated = dot_t(tokens[everything], gate[...])
        raised = dot_t(tokens[everything], up[...])
        active[everything] = (gated / (1.0 + jnp.exp(-gated)) * raised).astype(BF16)
        if part + 1 < len(PARTS):
            receive(part + 1)

        def step(k, carry):
            @pl.when(k < STEPS)
            def _():
                block = flipped(me // 4, k, 3)
                cut = pl.ds(pl.multiple_of(block * COLS, COLS), COLS)
                total = dot(active[everything], down[:, cut])
                at = pl.ds(first_group * STEPS + k * count, count)

                @pl.when(core == 0)
                def _():
                    kept[k, :rows] = total[:rows]
                    partial_out[at] = total[rows:].astype(BF16).reshape(count, OWN, COLS)

                @pl.when(core == 1)
                def _():
                    kept[k, :rows] = total[rows:]
                    partial_out[at] = total[:rows].astype(BF16).reshape(count, OWN, COLS)

                sem = part * STEPS + k
                remote(
                    partial_out.at[at], partial_in.at[at], partial_send.at[sem], partial_recv.at[sem], me, partner
                ).start()

            @pl.when(k >= LAG)
            def _():
                late = k - LAG
                block = flipped(me // 4, late, 3)
                at = pl.ds(first_group * STEPS + late * count, count)
                wait_bytes(partial_in.at[at], partial_recv.at[part * STEPS + late])
                other = partial_in[at].reshape(rows, COLS).astype(F32)
                total = (kept[late, :rows] + other).astype(BF16)
                base = block * 4
                for where in (0, 1):
                    for q in range(4):
                        returning[base + where * WIDE + q, first_group : first_group + count] = total[
                            where * size : (where + 1) * size, q * LANE : (q + 1) * LANE
                        ].reshape(count, GROUP_SLOTS, LANE)
                for q in range(4):
                    spot = flipped(me % 4, q, 2)
                    target = block * 4 + spot
                    for turn in (0, 1):
                        where = high if turn == 0 else 1 - high
                        slot = returning.at[base + where * WIDE + spot, groups]
                        home = returned.at[high * WIDE + me, groups]
                        sems = back_send.at[part], back_recv.at[part, high]
                        if turn == 1 or q > 0:
                            remote(slot, home, *sems, target, where * 2 + core).start()
                        else:

                            @pl.when(late > 0)
                            def _():
                                remote(slot, home, *sems, target, where * 2 + core).start()

                            @pl.when(late == 0)
                            def _():
                                pltpu.make_async_copy(slot, home, local_sem.at[11 + part]).start()

            return carry

        lax.fori_loop(0, STEPS + LAG, step, 0)

    def combine(part):
        first_group, count = PARTS[part]
        groups = pl.ds(first_group, count)
        wait_bytes(returned.at[0, groups], local_sem.at[11 + part])
        wait_bytes(returned.at[pl.ds(0, WIDE - 1), groups], back_recv.at[part, high])
        wait_bytes(returned.at[pl.ds(0, WIDE), groups], back_recv.at[part, 1 - high])
        for g in range(first_group, first_group + count):
            picks = [jnp.zeros((LANE, LANE), F32)] * 2
            for where in (0, 1):
                for s in (0, 1):
                    rows = jnp.concatenate([returned[where * WIDE + 2 * e + s, g] for e in range(EXPERTS)], axis=0)
                    picks = [picks[k] + dot(placed[g, k], rows) for k in (0, 1)]
            weight = to_column(heavy[g : g + 1])
            result[g * LANE : (g + 1) * LANE] = (
                residual[g * LANE : (g + 1) * LANE].astype(F32) + weight * picks[0] + (1.0 - weight) * picks[1]
            ).astype(BF16)

    receive(0)
    for load in loads:
        load.wait()
    experts(0)
    experts(1)

    collect(stats, stats_in, 0)
    averages = jnp.zeros((GROUPS, LANE), F32)
    for w in range(WIDE):
        averages += stats_in[w, :GROUPS]
    averages = averages * (1.0 / WIDE)
    squares = jnp.zeros((GROUPS, LANE), F32)
    for w in range(WIDE):
        shift = stats_in[w, :GROUPS] - averages
        squares += stats_in[w, GROUPS:] + LANE * (shift * shift)
    scales = lax.rsqrt(squares * (1.0 / D) + EPS)
    own_gain = gain_two[pl.ds(me, 1), :]
    own_router = router[:, pl.ds(pl.multiple_of(me * LANE, LANE), LANE)]
    for g in range(GROUPS):
        values = residual[g * LANE : (g + 1) * LANE].astype(F32)
        here = ((values - to_column(averages[g : g + 1])) * to_column(scales[g : g + 1]) * own_gain).astype(BF16)
        logits = dot_t(here, own_router)
        pair = named(g)
        lead = jnp.sum(
            jnp.where(expert_ids == pair[0], logits, 0.0) - jnp.where(expert_ids == pair[1], logits, 0.0),
            axis=1,
            keepdims=True,
        )
        diffs[g : g + 1, :] = to_row(lead)
        diffs[GROUPS + g : GROUPS + g + 1, :] = jnp.zeros((1, LANE), F32)
    share(diffs, diffs_in, 1)
    experts(2)

    collect(diffs, diffs_in, 1)
    leads = jnp.zeros((GROUPS, LANE), F32)
    for w in range(WIDE):
        leads += diffs_in[w, :GROUPS]
    heavy = 1.0 / (1.0 + jnp.exp(-leads))
    for part in range(len(PARTS)):
        combine(part)

    spread.finish()
    spread2.finish()
    for swap in swaps:
        swap.wait_send()
    for which in range(2):
        wait_bytes(columns.at[0, pl.ds(0, WIDE - 1)], column_send.at[which])
        wait_bytes(stats_in.at[pl.ds(0, WIDE - 1)], small_send.at[which])
    for half in (0, 1):

        def sent(order, half=half):
            wait_bytes(fresh(parity, n, half), kv_send.at[half, order])

        sent(0)

        @pl.when(high == 0)
        def _():
            sent(1)
            sent(2)

        @pl.when(core == 0)
        def _():
            sent(3)
            sent(4)

        @pl.when(high == 1)
        def _():
            sent(5)
            sent(6)

    for part, (first_group, count) in enumerate(PARTS):
        groups = pl.ds(first_group, count)
        wait_bytes(arrived.at[pl.ds(0, 2 * WIDE - 1), groups], out_send.at[part])
        wait_bytes(returned.at[pl.ds(0, 2 * WIDE - 1), groups], back_send.at[part])
        for k in range(STEPS):
            wait_bytes(partial_out.at[pl.ds(0, count)], partial_send.at[part * STEPS + k])


def body(
    hidden,
    attn_gain,
    query_weight,
    key_weight,
    value_weight,
    out_weight,
    cache_key,
    cache_value,
    mlp_gain,
    router_weight,
    expert_ids,
    gate_weight,
    up_weight,
    down_weight,
):
    anywhere = pl.BlockSpec(memory_space=pl.ANY)
    vmem = pl.BlockSpec(memory_space=pltpu.VMEM)
    dma = pltpu.SemaphoreType.DMA

    def held(*shape, kind=BF16):
        return pltpu.VMEM(shape, kind)

    return pl.pallas_call(
        layer_kernel,
        out_shape=jax.ShapeDtypeStruct((ROWS, LANE), BF16),
        in_specs=[anywhere, vmem] + [anywhere] * 6 + [vmem] * 3 + [anywhere] * 3,
        out_specs=vmem,
        scratch_shapes=[
            held(WIDE, ROWS, LANE),
            held(WIDE, ROWS, LANE),
            held(LANE, D),
            held(D, 2 * LANE),
            held(2, WIDE, LANE // 2, LANE),
            held(2, WIDE, LANE // 2, LANE),
            held(D, LANE),
            held(2, NARROW + 1, ROWS, LANE),
            held(ROWS, LANE),
            held(ROWS, LANE),
            held(ROWS, LANE),
            held(ROWS, LANE),
            held(ROWS, LANE, kind=F32),
            held(2, ROWS, LANE, kind=F32),
            held(ROWS, LANE, kind=F32),
            held(HIDDEN, D),
            held(HIDDEN, D),
            held(HIDDEN, D),
            held(2 * GROUPS, LANE, kind=F32),
            held(WIDE, 2 * GROUPS, LANE, kind=F32),
            held(2 * GROUPS, LANE, kind=F32),
            held(WIDE, 2 * GROUPS, LANE, kind=F32),
            held(GROUPS, 2, LANE, EXPERTS * GROUP_SLOTS),
            held(EXPERTS, GROUPS, GROUP_SLOTS, LANE),
            held(ALL, GROUPS, GROUP_SLOTS, LANE),
            held(2 * LANE, D),
            held(2 * LANE, HIDDEN),
            held(GROUPS * STEPS, OWN, COLS),
            held(GROUPS * STEPS, OWN, COLS),
            held(STEPS, LANE, COLS, kind=F32),
            held(2 * WIDE, GROUPS, GROUP_SLOTS, LANE),
            held(2 * WIDE, GROUPS, GROUP_SLOTS, LANE),
            dma((SENDS,)),
            dma((2, WIDE)),
            dma((SENDS,)),
            dma((2, WIDE)),
            dma((11 + len(PARTS),)),
            dma((2,)),
            dma((2,)),
            dma((4,)),
            dma((2, 7)),
            dma((2, 2, NARROW)),
            dma((3,)),
            dma((2,)),
            dma((2,)),
            dma((len(PARTS),)),
            dma((len(PARTS), 2)),
            dma((len(PARTS), 2)),
            dma((len(PARTS), 2)),
            dma((len(PARTS) * STEPS,)),
            dma((len(PARTS) * STEPS,)),
            dma((len(PARTS),)),
            dma((len(PARTS), 2)),
        ],
        compiler_params=pltpu.CompilerParams(
            collective_id=0, has_side_effects=True, vmem_limit_bytes=60 * 2**20
        ),
    )(
        hidden,
        attn_gain.reshape(WIDE, LANE),
        query_weight,
        key_weight,
        value_weight,
        out_weight,
        cache_key,
        cache_value,
        mlp_gain.reshape(WIDE, LANE),
        router_weight.T,
        expert_ids.T,
        gate_weight.swapaxes(1, 2),
        up_weight.swapaxes(1, 2),
        down_weight,
    )


def solution(mesh):
    placed = (
        P("narrow", "wide"),
        P(),
        P(None, "wide"),
        P("wide", None),
        P("wide", None),
        P("wide", None),
        P(),
        P(),
        P(),
        P(),
        P("narrow", None),
        P("wide", None, "narrow"),
        P("wide", None, "narrow"),
        P("wide", "narrow", None),
    )
    return jax.shard_map(
        body, mesh=mesh, in_specs=placed, out_specs=P("narrow", "wide"), check_vma=False
    )
```

```python
import jax
import jax.numpy as jnp
from jax import lax
from jax.experimental import pallas as pl
from jax.experimental.pallas import tpu as pltpu
from jax.sharding import PartitionSpec as P

MESH = pl.DeviceIdType.MESH
F32 = jnp.float32
BF16 = jnp.bfloat16

XN, YL, ZN = 4, 2, 4
WIDE = XN * YL * ZN
NARROW = 4
ROWS = 512
LANE = 128
D = WIDE * LANE
HALF = ROWS // 2
KV_SHARE = 4
EXPERTS = 16
CAP = 4
BLOCK = 16
HIDDEN = 800
EPS = 1e-5
SCALE = LANE**-0.5


def remote(src, dst, send_sem, recv_sem, wide, narrow):
    return pltpu.make_async_remote_copy(
        src_ref=src,
        dst_ref=dst,
        send_sem=send_sem,
        recv_sem=recv_sem,
        device_id=(wide, narrow),
        device_id_type=MESH,
    )


def wait_bytes(ref, sem):
    pltpu.make_async_copy(ref, ref, sem).wait()


def dot(a, b):
    return jnp.dot(a, b, preferred_element_type=F32)


def wide_of(x, y, z):
    return (x * YL + y) * ZN + z


def flipped(index, mask, bits):
    return sum(((index // 2**b + mask // 2**b) % 2) * 2**b for b in range(bits))


class Spread:
    def __init__(self, own, buf, me, narrow, send_sem, recv_sem, begin, visit):
        self.own, self.buf, self.me, self.narrow = own, buf, me, narrow
        self.begin, self.visit = begin, visit
        self.send_sem, self.recv_sem = send_sem, recv_sem
        self.x = me // (YL * ZN)
        self.y = (me // ZN) % YL
        self.z = me % ZN
        self.started = []

    def place(self, half, first, y, second):
        return wide_of(first, y, second) if half == 0 else wide_of(second, y, first)

    def coordinates(self, half):
        return (self.x, self.z) if half == 0 else (self.z, self.x)

    def send(self, half, block, target):
        rows = pl.ds(half * HALF, HALF)
        own = block is None
        slot = self.me if own else block
        copy = remote(
            self.own.at[rows] if own else self.buf.at[slot, rows],
            self.buf.at[slot, rows],
            self.send_sem.at[len(self.started)],
            self.recv_sem.at[half, slot],
            target,
            self.narrow,
        )
        copy.start()
        self.started.append(copy)

    def arrive(self, half, block):
        rows = pl.ds(half * HALF, HALF)
        wait_bytes(self.buf.at[block, rows], self.recv_sem.at[half, block])

    def around(self, half, block, dimension):
        first, second = self.coordinates(half)
        for step in (1, 3):
            if dimension == 0:
                target = self.place(half, (first + step) % 4, self.y, second)
            else:
                target = self.place(half, first, self.y, (second + step) % 4)
            self.send(half, block, target)

    def start(self):
        for half in (0, 1):
            first, second = self.coordinates(half)
            self.send(half, None, self.place(half, first, 1 - self.y, second))
        for half in (0, 1):
            self.around(half, None, 0)
        for half in (0, 1):
            self.around(half, None, 1)

    def run(self):
        for half in (0, 1):
            first, second = self.coordinates(half)
            block = self.place(half, first, 1 - self.y, second)
            self.arrive(half, block)
            self.around(half, block, 0)
            self.around(half, block, 1)
        self.begin()
        for half in (0, 1):
            first, second = self.coordinates(half)
            self.visit(self.place(half, first, 1 - self.y, second), half)
        for y in (0, 1):
            for step in (1, 3):
                for half in (0, 1):
                    first, second = self.coordinates(half)
                    block = self.place(half, (first + step) % 4, y, second)
                    self.arrive(half, block)
                    if (step == 3) == (y == 0):
                        opposite = (first + 4 - step) % 4
                        self.send(half, block, self.place(half, opposite, self.y, second))
                    self.around(half, block, 1)
                    self.visit(block, half)
        for y in (0, 1):
            for half in (0, 1):
                first, second = self.coordinates(half)
                block = self.place(half, (first + 2) % 4, y, second)
                self.arrive(half, block)
                self.around(half, block, 1)
                self.visit(block, half)
        for hop in (0, 1, 3, 2):
            for y in (0, 1):
                for step in (1, 3):
                    for half in (0, 1):
                        first, second = self.coordinates(half)
                        block = self.place(half, (first + hop) % 4, y, (second + step) % 4)
                        self.arrive(half, block)
                        if (step == 3) == (y == 0):
                            opposite = (second + 4 - step) % 4
                            self.send(half, block, self.place(half, first, self.y, opposite))
                        self.visit(block, half)
        for hop in (0, 1, 3, 2):
            for y in (0, 1):
                for half in (0, 1):
                    first, second = self.coordinates(half)
                    block = self.place(half, (first + hop) % 4, y, (second + 2) % 4)
                    self.arrive(half, block)
                    self.visit(block, half)

    def finish(self):
        for copy in self.started:
            copy.wait_send()


SENDS = 62


def greet(peers):
    barrier = pltpu.get_barrier_semaphore()
    for count, peer in peers:

        def one(i, carry, peer=peer):
            wide, narrow = peer(i)
            pl.semaphore_signal(barrier, inc=1, device_id=(wide, narrow), device_id_type=MESH)
            return carry

        lax.fori_loop(0, count, one, 0)
    pl.semaphore_wait(barrier, sum(count for count, _ in peers))


GROUPS = ROWS // LANE
GROUP_SLOTS = LANE // BLOCK * CAP
PARTS = ((0, 2), (2, 1), (3, 1))
OWN = 2 * GROUP_SLOTS
COLS = 512
STEPS = D // COLS
LAG = 4
BITS = 5
ALL = NARROW * WIDE


def dot_t(a, b):
    return lax.dot_general(a, b, (((1,), (1,)), ((), ())), preferred_element_type=F32)


def layer_kernel(
    hidden,
    gain,
    query_weight,
    key_weight,
    value_weight,
    out_weight,
    cache_key,
    cache_value,
    gain_two,
    router,
    ids,
    gate_weight,
    up_weight,
    down_weight,
    result,
    gathered,
    mixed,
    normed,
    joined,
    columns,
    out_columns,
    out_joined,
    kv,
    queries,
    attended,
    own_hidden,
    residual,
    shift,
    sums,
    mixture,
    gate,
    up,
    down,
    stats,
    stats_in,
    diffs,
    diffs_in,
    placed,
    outgoing,
    arrived,
    tokens,
    active,
    partial_out,
    partial_in,
    kept,
    returning,
    returned,
    spread_send,
    spread_recv,
    spread_send2,
    spread_recv2,
    local_sem,
    column_send,
    column_recv,
    pair_sem,
    kv_send,
    kv_recv,
    weight_sem,
    small_send,
    small_recv,
    out_send,
    out_recv,
    pair_send,
    pair_recv,
    partial_send,
    partial_recv,
    back_send,
    back_recv,
):
    me = lax.axis_index("wide")
    n = lax.axis_index("narrow")
    core = n % 2
    high = n // 2
    partner = n + 1 - 2 * core
    far = n + 2 - 4 * high
    across = far + 1 - 2 * core
    parity = me % 2
    group = me // KV_SHARE
    mate = me + 1 - 2 * parity

    locals_ = [
        pltpu.make_async_copy(hidden, gathered.at[me], local_sem.at[0]),
        pltpu.make_async_copy(query_weight, joined.at[:, pl.ds(0, LANE)], local_sem.at[1]),
        pltpu.make_async_copy(cache_key.at[group], kv.at[0, 0], local_sem.at[2]),
        pltpu.make_async_copy(cache_value.at[group], kv.at[1, 0], local_sem.at[3]),
        pltpu.make_async_copy(hidden, own_hidden, local_sem.at[4]),
    ]
    for copy in locals_:
        copy.start()
    loads = [
        pltpu.make_async_copy(gate_weight.at[0], gate, weight_sem.at[0]),
        pltpu.make_async_copy(up_weight.at[0], up, weight_sem.at[1]),
        pltpu.make_async_copy(down_weight.at[0], down, weight_sem.at[2]),
    ]

    greet(
        [
            (WIDE - 1, lambda i: ((me + 1 + i) % WIDE, n)),
            (WIDE, lambda i: ((me + i) % WIDE, far)),
            (2, lambda i: (me, partner + i * (across - partner))),
            (2, lambda i: (mate, partner + i * (across - partner))),
        ]
    )

    def gather_own():
        locals_[4].wait()
        own = own_hidden[...].astype(F32)
        shift[...] = jnp.broadcast_to(jnp.sum(own, axis=1, keepdims=True) * (1.0 / LANE), (ROWS, LANE))
        own = own - shift[...]
        sums[0] = own
        sums[1] = own * own

    def gather_sums(block, half):
        rows = slice(half * HALF, (half + 1) * HALF)
        moved = gathered[block, rows].astype(F32) - shift[rows]
        sums[0, rows] += moved
        sums[1, rows] += moved * moved

    spread = Spread(hidden, gathered, me, n, spread_send, spread_recv, gather_own, gather_sums)
    spread.start()

    half_rows = pl.ds(core * (LANE // 2), LANE // 2)

    def send_column(i, carry):
        target = flipped(me, i + 1, BITS)
        cut = pl.ds(pl.multiple_of((target // KV_SHARE) * LANE, LANE), LANE)

        @pl.when(target % 2 == 0)
        def _():
            remote(
                key_weight.at[half_rows, cut], columns.at[core, me], column_send.at[0], column_recv.at[0], target, n
            ).start()

        @pl.when(target % 2 == 1)
        def _():
            remote(
                value_weight.at[half_rows, cut], columns.at[core, me], column_send.at[0], column_recv.at[0], target, n
            ).start()

        return carry

    lax.fori_loop(0, WIDE - 1, send_column, 0)
    own_cut = pl.ds(pl.multiple_of(group * LANE, LANE), LANE)

    @pl.when(parity == 0)
    def _():
        pltpu.make_async_copy(key_weight.at[half_rows, own_cut], columns.at[core, me], local_sem.at[5]).start()

    @pl.when(parity == 1)
    def _():
        pltpu.make_async_copy(value_weight.at[half_rows, own_cut], columns.at[core, me], local_sem.at[5]).start()

    spread.run()
    for load in loads:
        load.start()

    wait_bytes(columns.at[core, me], local_sem.at[5])
    wait_bytes(columns.at[0, pl.ds(0, WIDE - 1)], column_recv.at[0])
    swap = remote(columns.at[core], columns.at[core], pair_sem.at[0], pair_sem.at[1], me, partner)
    swap.start()

    def send_out_column(i, carry):
        target = flipped(me, i + 1, BITS)
        cut = pl.ds(pl.multiple_of(target * LANE, LANE), LANE)
        remote(
            out_weight.at[half_rows, cut], out_columns.at[core, me], column_send.at[1], column_recv.at[1], target, n
        ).start()
        return carry

    lax.fori_loop(0, WIDE - 1, send_out_column, 0)
    own_out = pltpu.make_async_copy(
        out_weight.at[half_rows, pl.ds(pl.multiple_of(me * LANE, LANE), LANE)], out_columns.at[core, me], local_sem.at[6]
    )
    own_out.start()

    for copy in locals_[:4]:
        copy.wait()

    swap.wait()
    for half in (0, 1):
        for w in range(WIDE):
            joined[w * LANE + half * (LANE // 2) : w * LANE + (half + 1) * (LANE // 2), LANE:] = columns[half, w]

    def project(tile, carry):
        rows = pl.ds(pl.multiple_of(tile * LANE, LANE), LANE)
        offset = jnp.sum(sums[0, rows], axis=1, keepdims=True) * (1.0 / D)
        square = jnp.sum(sums[1, rows], axis=1, keepdims=True) * (1.0 / D)
        average = jnp.max(shift[rows], axis=1, keepdims=True) + offset
        scale = lax.rsqrt(jnp.maximum(square - offset * offset, 0.0) + EPS)
        for w in range(WIDE):
            centered = gathered[w, rows].astype(F32) - average
            normed[:, w * LANE : (w + 1) * LANE] = (centered * scale * gain[w : w + 1, :]).astype(BF16)
        product = dot(normed[...], joined[...]).astype(BF16)
        queries[rows] = product[:, :LANE]
        kv[parity, n + 1, rows] = product[:, LANE:]
        return carry

    def fresh(kind, block, half):
        return kv.at[kind, block + 1, pl.ds(half * HALF, HALF)]

    def give(kind, half, block, order, wide, narrow):
        piece = fresh(kind, block, half)
        remote(piece, piece, kv_send.at[half, order], kv_recv.at[kind, half, block], wide, narrow).start()

    def take(kind, half, block):
        wait_bytes(fresh(kind, block, half), kv_recv.at[kind, half, block])

    for half in (0, 1):
        lax.fori_loop(half * 2, half * 2 + 2, project, 0)
        give(parity, half, n, 0, mate, n)

        @pl.when(high == 0)
        def _():
            give(parity, half, n, 1, me, far)
            give(parity, half, n, 2, mate, far)

        @pl.when(core == 0)
        def _():
            give(parity, half, n, 3, me, partner)

    row_ids = lax.broadcasted_iota(jnp.int32, (ROWS, ROWS), 0)
    key_ids = lax.broadcasted_iota(jnp.int32, (ROWS, ROWS), 1)
    causal = key_ids <= row_ids

    def attend(j, state):
        highest, total, acc = state
        scores = dot_t(queries[...], kv[0, j]) * SCALE
        scores = jnp.where(jnp.logical_or(causal, j <= n), scores, -1e30)
        new = jnp.maximum(highest, jnp.max(scores, axis=1, keepdims=True))
        weights = jnp.exp(scores - new)
        fade = jnp.exp(highest - new)
        total = total * fade + jnp.sum(weights, axis=1, keepdims=True)
        acc = acc * fade + dot(weights.astype(BF16), kv[1, j])
        return new, total, acc

    state = (
        jnp.full((ROWS, 1), -1e30, F32),
        jnp.zeros((ROWS, 1), F32),
        jnp.zeros((ROWS, LANE), F32),
    )
    state = lax.fori_loop(0, 1, attend, state)
    own_out.wait()
    wait_bytes(out_columns.at[0, pl.ds(0, WIDE - 1)], column_recv.at[1])
    swap_out = remote(out_columns.at[core], out_columns.at[core], pair_sem.at[2], pair_sem.at[3], me, partner)
    swap_out.start()
    for half in (0, 1):
        take(1 - parity, half, n)

        @pl.when(core == 0)
        def _():
            give(1 - parity, half, n, 4, me, partner)

        @pl.when(high == 1)
        def _():
            take(parity, half, far)
            give(parity, half, far, 5, me, partner)
            take(1 - parity, half, far)
            give(1 - parity, half, far, 6, me, partner)

    eye = (
        lax.broadcasted_iota(jnp.int32, (LANE, LANE), 0) == lax.broadcasted_iota(jnp.int32, (LANE, LANE), 1)
    ).astype(F32)

    def to_row(column):
        return jnp.sum(column * eye, axis=0, keepdims=True)

    def to_column(row):
        return jnp.sum(row * eye, axis=1, keepdims=True)

    below = lax.broadcasted_iota(jnp.int32, (LANE, LANE), 0)
    left = lax.broadcasted_iota(jnp.int32, (LANE, LANE), 1)
    earlier = jnp.logical_and(left < below, left // BLOCK == below // BLOCK).astype(BF16)
    expert_ids = lax.broadcasted_iota(jnp.int32, (LANE, EXPERTS), 1)
    slot_ids = lax.broadcasted_iota(jnp.int32, (LANE, EXPERTS * GROUP_SLOTS), 1)
    in_group = lax.broadcasted_iota(jnp.int32, (LANE, 1), 0) // BLOCK * CAP

    def named(g):
        return [
            to_column(ids[k : k + 1, g * LANE : (g + 1) * LANE].astype(F32)).astype(jnp.int32) for k in (0, 1)
        ]

    for g in range(GROUPS):
        pair = named(g)
        hot = [expert_ids == chosen for chosen in pair]
        before = dot(earlier, jnp.logical_or(hot[0], hot[1]).astype(BF16))
        for k in (0, 1):
            position = jnp.sum(jnp.where(hot[k], before, 0.0), axis=1, keepdims=True).astype(jnp.int32)
            slot = pair[k] * GROUP_SLOTS + in_group + position
            placed[g, k] = (slot_ids == slot).astype(BF16)

    swap_out.wait()
    for half in (0, 1):
        for w in range(WIDE):
            out_joined[w * LANE + half * (LANE // 2) : w * LANE + (half + 1) * (LANE // 2), :] = out_columns[half, w]

    for half in (0, 1):

        @pl.when(core == 1)
        def _():
            take(parity, half, partner)
            take(1 - parity, half, partner)

        @pl.when(high == 1)
        def _():
            take(parity, half, across)
            take(1 - parity, half, across)

    _, total, acc = lax.fori_loop(1, n + 2, attend, state)
    attended[...] = (acc / total).astype(BF16)

    def out_rows(block):
        return out_joined[pl.ds(pl.multiple_of(block * LANE, LANE), LANE), :]

    def mix_own():
        mixture[...] = own_hidden[...].astype(F32) + dot(attended[...], out_rows(me))

    def gather_products(block, half):
        rows = slice(half * HALF, (half + 1) * HALF)
        mixture[rows] += dot(mixed[block, rows], out_rows(block))

    spread2 = Spread(attended, mixed, me, n, spread_send2, spread_recv2, mix_own, gather_products)
    spread2.start()

    spread2.run()

    def dispatch(part):
        groups = pl.ds(*PARTS[part])
        slot = arrived.at[n * WIDE + me, groups]

        def one(i, carry):
            target = flipped(me, i, BITS)
            source = outgoing.at[target // 2, groups]

            @pl.when(i > 0)
            def _():
                remote(source, slot, out_send.at[part], out_recv.at[part, high], target, n).start()

            remote(source, slot, out_send.at[part], out_recv.at[part, high], target, far).start()
            return carry

        lax.fori_loop(0, WIDE, one, 0)
        pltpu.make_async_copy(outgoing.at[me // 2, groups], slot, local_sem.at[8 + part]).start()

    def share(mine, everyone, which):
        def one(i, carry):
            target = flipped(me, i + 1, BITS)
            remote(mine, everyone.at[me], small_send.at[which], small_recv.at[which], target, n).start()
            return carry

        lax.fori_loop(0, WIDE - 1, one, 0)

    def collect(mine, everyone, which):
        everyone[me] = mine[...]
        wait_bytes(everyone.at[pl.ds(0, WIDE - 1)], small_recv.at[which])

    def deviations_of(g):
        values = residual[g * LANE : (g + 1) * LANE].astype(F32)
        average = jnp.sum(values, axis=1, keepdims=True) * (1.0 / LANE)
        centered = values - average
        deviations = jnp.sum(centered * centered, axis=1, keepdims=True)
        stats[g : g + 1, :] = to_row(average)
        stats[GROUPS + g : GROUPS + g + 1, :] = to_row(deviations)

    for part, (first_group, count) in enumerate(PARTS):
        for g in range(first_group, first_group + count):
            rows = slice(g * LANE, (g + 1) * LANE)
            here = mixture[rows].astype(BF16)
            residual[rows] = here
            filled = lax.dot_general(
                placed[g, 0] + placed[g, 1], here, (((0,), (0,)), ((), ())), preferred_element_type=F32
            ).astype(BF16)
            outgoing[:, g] = filled.reshape(EXPERTS, GROUP_SLOTS, LANE)
        dispatch(part)
        if part == 0:
            for g in range(GROUPS):
                residual[g * LANE : (g + 1) * LANE] = mixture[g * LANE : (g + 1) * LANE].astype(BF16)
                deviations_of(g)
            share(stats, stats_in, 0)

    def norm_tokens(part, source):
        first_group, count = PARTS[part]
        size = count * GROUP_SLOTS

        def values(w):
            block = arrived[source * WIDE + w, first_group : first_group + count]
            return block.reshape(size, LANE).astype(F32)

        total = jnp.zeros((size, LANE), F32)
        for w in range(WIDE):
            total += values(w)
        average = jnp.sum(total, axis=1, keepdims=True) * (1.0 / D)
        total = jnp.zeros((size, LANE), F32)
        for w in range(WIDE):
            centered = values(w) - average
            total += centered * centered
        scale = lax.rsqrt(jnp.sum(total, axis=1, keepdims=True) * (1.0 / D) + EPS)
        where = pl.ds(pl.multiple_of(((source % 2) * 2 + source // 2) * size, GROUP_SLOTS), size)
        for w in range(WIDE):
            centered = values(w) - average
            tokens[where, w * LANE : (w + 1) * LANE] = (centered * scale * gain_two[w : w + 1, :]).astype(BF16)

    swaps = []

    def receive(part):
        groups = pl.ds(*PARTS[part])
        wait_bytes(outgoing.at[0, groups], local_sem.at[8 + part])
        for order, where in enumerate((high, 1 - high)):
            blocks = WIDE - 1 if order == 0 else WIDE
            wait_bytes(arrived.at[pl.ds(0, blocks), groups], out_recv.at[part, where])
            piece = arrived.at[pl.ds((where * 2 + core) * WIDE, WIDE), groups]
            swap = remote(piece, piece, pair_send.at[part, where], pair_recv.at[part, where], me, partner)
            swap.start()
            swaps.append(swap)

    def experts(part):
        first_group, count = PARTS[part]
        groups = pl.ds(first_group, count)
        size = count * GROUP_SLOTS
        rows = count * OWN
        everything = pl.ds(0, 2 * rows)
        for where in (0, 1):
            norm_tokens(part, where * 2 + core)
        for where in (0, 1):
            wait_bytes(arrived.at[pl.ds(0, WIDE), groups], pair_recv.at[part, where])
            norm_tokens(part, where * 2 + 1 - core)
        gated = dot_t(tokens[everything], gate[...])
        raised = dot_t(tokens[everything], up[...])
        active[everything] = (gated / (1.0 + jnp.exp(-gated)) * raised).astype(BF16)
        if part + 1 < len(PARTS):
            receive(part + 1)

        def step(k, carry):
            @pl.when(k < STEPS)
            def _():
                block = flipped(me // 4, k, 3)
                cut = pl.ds(pl.multiple_of(block * COLS, COLS), COLS)
                total = dot(active[everything], down[:, cut])
                at = pl.ds(first_group * STEPS + k * count, count)

                @pl.when(core == 0)
                def _():
                    kept[k, :rows] = total[:rows]
                    partial_out[at] = total[rows:].astype(BF16).reshape(count, OWN, COLS)

                @pl.when(core == 1)
                def _():
                    kept[k, :rows] = total[rows:]
                    partial_out[at] = total[:rows].astype(BF16).reshape(count, OWN, COLS)

                sem = part * STEPS + k
                remote(
                    partial_out.at[at], partial_in.at[at], partial_send.at[sem], partial_recv.at[sem], me, partner
                ).start()

            @pl.when(k >= LAG)
            def _():
                late = k - LAG
                block = flipped(me // 4, late, 3)
                at = pl.ds(first_group * STEPS + late * count, count)
                wait_bytes(partial_in.at[at], partial_recv.at[part * STEPS + late])
                other = partial_in[at].reshape(rows, COLS).astype(F32)
                total = (kept[late, :rows] + other).astype(BF16)
                base = block * 4
                for where in (0, 1):
                    for q in range(4):
                        returning[base + where * WIDE + q, first_group : first_group + count] = total[
                            where * size : (where + 1) * size, q * LANE : (q + 1) * LANE
                        ].reshape(count, GROUP_SLOTS, LANE)
                for q in range(4):
                    spot = flipped(me % 4, q, 2)
                    target = block * 4 + spot
                    for turn in (0, 1):
                        where = high if turn == 0 else 1 - high
                        slot = returning.at[base + where * WIDE + spot, groups]
                        home = returned.at[high * WIDE + me, groups]
                        sems = back_send.at[part], back_recv.at[part, high]
                        if turn == 1 or q > 0:
                            remote(slot, home, *sems, target, where * 2 + core).start()
                        else:

                            @pl.when(late > 0)
                            def _():
                                remote(slot, home, *sems, target, where * 2 + core).start()

                            @pl.when(late == 0)
                            def _():
                                pltpu.make_async_copy(slot, home, local_sem.at[11 + part]).start()

            return carry

        lax.fori_loop(0, STEPS + LAG, step, 0)

    def combine(part):
        first_group, count = PARTS[part]
        groups = pl.ds(first_group, count)
        wait_bytes(returned.at[0, groups], local_sem.at[11 + part])
        wait_bytes(returned.at[pl.ds(0, WIDE - 1), groups], back_recv.at[part, high])
        wait_bytes(returned.at[pl.ds(0, WIDE), groups], back_recv.at[part, 1 - high])
        for g in range(first_group, first_group + count):
            picks = [jnp.zeros((LANE, LANE), F32)] * 2
            for where in (0, 1):
                for s in (0, 1):
                    rows = jnp.concatenate([returned[where * WIDE + 2 * e + s, g] for e in range(EXPERTS)], axis=0)
                    picks = [picks[k] + dot(placed[g, k], rows) for k in (0, 1)]
            weight = to_column(heavy[g : g + 1])
            result[g * LANE : (g + 1) * LANE] = (
                residual[g * LANE : (g + 1) * LANE].astype(F32) + weight * picks[0] + (1.0 - weight) * picks[1]
            ).astype(BF16)

    receive(0)
    for load in loads:
        load.wait()
    experts(0)
    experts(1)

    collect(stats, stats_in, 0)
    averages = jnp.zeros((GROUPS, LANE), F32)
    for w in range(WIDE):
        averages += stats_in[w, :GROUPS]
    averages = averages * (1.0 / WIDE)
    squares = jnp.zeros((GROUPS, LANE), F32)
    for w in range(WIDE):
        shift = stats_in[w, :GROUPS] - averages
        squares += stats_in[w, GROUPS:] + LANE * (shift * shift)
    scales = lax.rsqrt(squares * (1.0 / D) + EPS)
    own_gain = gain_two[pl.ds(me, 1), :]
    own_router = router[:, pl.ds(pl.multiple_of(me * LANE, LANE), LANE)]
    for g in range(GROUPS):
        values = residual[g * LANE : (g + 1) * LANE].astype(F32)
        here = ((values - to_column(averages[g : g + 1])) * to_column(scales[g : g + 1]) * own_gain).astype(BF16)
        logits = dot_t(here, own_router)
        pair = named(g)
        lead = jnp.sum(
            jnp.where(expert_ids == pair[0], logits, 0.0) - jnp.where(expert_ids == pair[1], logits, 0.0),
            axis=1,
            keepdims=True,
        )
        diffs[g : g + 1, :] = to_row(lead)
        diffs[GROUPS + g : GROUPS + g + 1, :] = jnp.zeros((1, LANE), F32)
    share(diffs, diffs_in, 1)
    experts(2)

    collect(diffs, diffs_in, 1)
    leads = jnp.zeros((GROUPS, LANE), F32)
    for w in range(WIDE):
        leads += diffs_in[w, :GROUPS]
    heavy = 1.0 / (1.0 + jnp.exp(-leads))
    for part in range(len(PARTS)):
        combine(part)

    spread.finish()
    spread2.finish()
    for swap in swaps:
        swap.wait_send()
    for which in range(2):
        wait_bytes(columns.at[0, pl.ds(0, WIDE - 1)], column_send.at[which])
        wait_bytes(stats_in.at[pl.ds(0, WIDE - 1)], small_send.at[which])
    for half in (0, 1):

        def sent(order, half=half):
            wait_bytes(fresh(parity, n, half), kv_send.at[half, order])

        sent(0)

        @pl.when(high == 0)
        def _():
            sent(1)
            sent(2)

        @pl.when(core == 0)
        def _():
            sent(3)
            sent(4)

        @pl.when(high == 1)
        def _():
            sent(5)
            sent(6)

    for part, (first_group, count) in enumerate(PARTS):
        groups = pl.ds(first_group, count)
        wait_bytes(arrived.at[pl.ds(0, 2 * WIDE - 1), groups], out_send.at[part])
        wait_bytes(returned.at[pl.ds(0, 2 * WIDE - 1), groups], back_send.at[part])
        for k in range(STEPS):
            wait_bytes(partial_out.at[pl.ds(0, count)], partial_send.at[part * STEPS + k])


def body(
    hidden,
    attn_gain,
    query_weight,
    key_weight,
    value_weight,
    out_weight,
    cache_key,
    cache_value,
    mlp_gain,
    router_weight,
    expert_ids,
    gate_weight,
    up_weight,
    down_weight,
):
    anywhere = pl.BlockSpec(memory_space=pl.ANY)
    vmem = pl.BlockSpec(memory_space=pltpu.VMEM)
    dma = pltpu.SemaphoreType.DMA

    def held(*shape, kind=BF16):
        return pltpu.VMEM(shape, kind)

    return pl.pallas_call(
        layer_kernel,
        out_shape=jax.ShapeDtypeStruct((ROWS, LANE), BF16),
        in_specs=[anywhere, vmem] + [anywhere] * 6 + [vmem] * 3 + [anywhere] * 3,
        out_specs=vmem,
        scratch_shapes=[
            held(WIDE, ROWS, LANE),
            held(WIDE, ROWS, LANE),
            held(LANE, D),
            held(D, 2 * LANE),
            held(2, WIDE, LANE // 2, LANE),
            held(2, WIDE, LANE // 2, LANE),
            held(D, LANE),
            held(2, NARROW + 1, ROWS, LANE),
            held(ROWS, LANE),
            held(ROWS, LANE),
            held(ROWS, LANE),
            held(ROWS, LANE),
            held(ROWS, LANE, kind=F32),
            held(2, ROWS, LANE, kind=F32),
            held(ROWS, LANE, kind=F32),
            held(HIDDEN, D),
            held(HIDDEN, D),
            held(HIDDEN, D),
            held(2 * GROUPS, LANE, kind=F32),
            held(WIDE, 2 * GROUPS, LANE, kind=F32),
            held(2 * GROUPS, LANE, kind=F32),
            held(WIDE, 2 * GROUPS, LANE, kind=F32),
            held(GROUPS, 2, LANE, EXPERTS * GROUP_SLOTS),
            held(EXPERTS, GROUPS, GROUP_SLOTS, LANE),
            held(ALL, GROUPS, GROUP_SLOTS, LANE),
            held(2 * LANE, D),
            held(2 * LANE, HIDDEN),
            held(GROUPS * STEPS, OWN, COLS),
            held(GROUPS * STEPS, OWN, COLS),
            held(STEPS, LANE, COLS, kind=F32),
            held(2 * WIDE, GROUPS, GROUP_SLOTS, LANE),
            held(2 * WIDE, GROUPS, GROUP_SLOTS, LANE),
            dma((SENDS,)),
            dma((2, WIDE)),
            dma((SENDS,)),
            dma((2, WIDE)),
            dma((11 + len(PARTS),)),
            dma((2,)),
            dma((2,)),
            dma((4,)),
            dma((2, 7)),
            dma((2, 2, NARROW)),
            dma((3,)),
            dma((2,)),
            dma((2,)),
            dma((len(PARTS),)),
            dma((len(PARTS), 2)),
            dma((len(PARTS), 2)),
            dma((len(PARTS), 2)),
            dma((len(PARTS) * STEPS,)),
            dma((len(PARTS) * STEPS,)),
            dma((len(PARTS),)),
            dma((len(PARTS), 2)),
        ],
        compiler_params=pltpu.CompilerParams(
            collective_id=0, has_side_effects=True, vmem_limit_bytes=60 * 2**20
        ),
    )(
        hidden,
        attn_gain.reshape(WIDE, LANE),
        query_weight,
        key_weight,
        value_weight,
        out_weight,
        cache_key,
        cache_value,
        mlp_gain.reshape(WIDE, LANE),
        router_weight.T,
        expert_ids.T,
        gate_weight.swapaxes(1, 2),
        up_weight.swapaxes(1, 2),
        down_weight,
    )


def solution(mesh):
    placed = (
        P("narrow", "wide"),
        P(),
        P(None, "wide"),
        P("wide", None),
        P("wide", None),
        P("wide", None),
        P(),
        P(),
        P(),
        P(),
        P("narrow", None),
        P("wide", None, "narrow"),
        P("wide", None, "narrow"),
        P("wide", "narrow", None),
    )
    return jax.shard_map(
        body, mesh=mesh, in_specs=placed, out_specs=P("narrow", "wide"), check_vma=False
    )
```

```python
import jax
import jax.numpy as jnp
from jax import lax
from jax.experimental import pallas as pl
from jax.experimental.pallas import tpu as pltpu
from jax.sharding import PartitionSpec as P

MESH = pl.DeviceIdType.MESH
F32 = jnp.float32
BF16 = jnp.bfloat16

XN, YL, ZN = 4, 2, 4
WIDE = XN * YL * ZN
NARROW = 4
ROWS = 512
LANE = 128
D = WIDE * LANE
HALF = ROWS // 2
KV_SHARE = 4
EXPERTS = 16
CAP = 4
BLOCK = 16
HIDDEN = 800
EPS = 1e-5
SCALE = LANE**-0.5


def remote(src, dst, send_sem, recv_sem, wide, narrow):
    return pltpu.make_async_remote_copy(
        src_ref=src,
        dst_ref=dst,
        send_sem=send_sem,
        recv_sem=recv_sem,
        device_id=(wide, narrow),
        device_id_type=MESH,
    )


def wait_bytes(ref, sem):
    pltpu.make_async_copy(ref, ref, sem).wait()


def dot(a, b):
    return jnp.dot(a, b, preferred_element_type=F32)


def wide_of(x, y, z):
    return (x * YL + y) * ZN + z


def flipped(index, mask, bits):
    return sum(((index // 2**b + mask // 2**b) % 2) * 2**b for b in range(bits))


class Spread:
    def __init__(self, own, buf, me, narrow, send_sem, recv_sem, begin, visit):
        self.own, self.buf, self.me, self.narrow = own, buf, me, narrow
        self.begin, self.visit = begin, visit
        self.send_sem, self.recv_sem = send_sem, recv_sem
        self.x = me // (YL * ZN)
        self.y = (me // ZN) % YL
        self.z = me % ZN
        self.started = []

    def place(self, half, first, y, second):
        return wide_of(first, y, second) if half == 0 else wide_of(second, y, first)

    def coordinates(self, half):
        return (self.x, self.z) if half == 0 else (self.z, self.x)

    def send(self, half, block, target):
        rows = pl.ds(half * HALF, HALF)
        own = block is None
        slot = self.me if own else block
        copy = remote(
            self.own.at[rows] if own else self.buf.at[slot, rows],
            self.buf.at[slot, rows],
            self.send_sem.at[len(self.started)],
            self.recv_sem.at[half, slot],
            target,
            self.narrow,
        )
        copy.start()
        self.started.append(copy)

    def arrive(self, half, block):
        rows = pl.ds(half * HALF, HALF)
        wait_bytes(self.buf.at[block, rows], self.recv_sem.at[half, block])

    def around(self, half, block, dimension):
        first, second = self.coordinates(half)
        for step in (1, 3):
            if dimension == 0:
                target = self.place(half, (first + step) % 4, self.y, second)
            else:
                target = self.place(half, first, self.y, (second + step) % 4)
            self.send(half, block, target)

    def start(self):
        for half in (0, 1):
            first, second = self.coordinates(half)
            self.send(half, None, self.place(half, first, 1 - self.y, second))
        for half in (0, 1):
            self.around(half, None, 0)
        for half in (0, 1):
            self.around(half, None, 1)

    def run(self):
        for half in (0, 1):
            first, second = self.coordinates(half)
            block = self.place(half, first, 1 - self.y, second)
            self.arrive(half, block)
            self.around(half, block, 0)
            self.around(half, block, 1)
        self.begin()
        for half in (0, 1):
            first, second = self.coordinates(half)
            self.visit(self.place(half, first, 1 - self.y, second), half)
        for y in (0, 1):
            for step in (1, 3):
                for half in (0, 1):
                    first, second = self.coordinates(half)
                    block = self.place(half, (first + step) % 4, y, second)
                    self.arrive(half, block)
                    if (step == 3) == (y == 0):
                        opposite = (first + 4 - step) % 4
                        self.send(half, block, self.place(half, opposite, self.y, second))
                    self.around(half, block, 1)
                    self.visit(block, half)
        for y in (0, 1):
            for half in (0, 1):
                first, second = self.coordinates(half)
                block = self.place(half, (first + 2) % 4, y, second)
                self.arrive(half, block)
                self.around(half, block, 1)
                self.visit(block, half)
        for hop in (0, 1, 3, 2):
            for y in (0, 1):
                for step in (1, 3):
                    for half in (0, 1):
                        first, second = self.coordinates(half)
                        block = self.place(half, (first + hop) % 4, y, (second + step) % 4)
                        self.arrive(half, block)
                        if (step == 3) == (y == 0):
                            opposite = (second + 4 - step) % 4
                            self.send(half, block, self.place(half, first, self.y, opposite))
                        self.visit(block, half)
        for hop in (0, 1, 3, 2):
            for y in (0, 1):
                for half in (0, 1):
                    first, second = self.coordinates(half)
                    block = self.place(half, (first + hop) % 4, y, (second + 2) % 4)
                    self.arrive(half, block)
                    self.visit(block, half)

    def finish(self):
        for copy in self.started:
            copy.wait_send()


SENDS = 62


def greet(peers):
    barrier = pltpu.get_barrier_semaphore()
    for count, peer in peers:

        def one(i, carry, peer=peer):
            wide, narrow = peer(i)
            pl.semaphore_signal(barrier, inc=1, device_id=(wide, narrow), device_id_type=MESH)
            return carry

        lax.fori_loop(0, count, one, 0)
    pl.semaphore_wait(barrier, sum(count for count, _ in peers))


GROUPS = ROWS // LANE
GROUP_SLOTS = LANE // BLOCK * CAP
PARTS = ((0, 2), (2, 1), (3, 1))
OWN = 2 * GROUP_SLOTS
COLS = 512
STEPS = D // COLS
LAG = 4
BITS = 5
ALL = NARROW * WIDE


def dot_t(a, b):
    return lax.dot_general(a, b, (((1,), (1,)), ((), ())), preferred_element_type=F32)


def layer_kernel(
    hidden,
    gain,
    query_weight,
    key_weight,
    value_weight,
    out_weight,
    cache_key,
    cache_value,
    gain_two,
    router,
    ids,
    gate_weight,
    up_weight,
    down_weight,
    result,
    gathered,
    mixed,
    normed,
    joined,
    columns,
    out_columns,
    out_joined,
    kv,
    queries,
    attended,
    own_hidden,
    residual,
    shift,
    sums,
    mixture,
    gate,
    up,
    down,
    stats,
    stats_in,
    diffs,
    diffs_in,
    placed,
    outgoing,
    arrived,
    tokens,
    active,
    partial_out,
    partial_in,
    kept,
    returning,
    returned,
    spread_send,
    spread_recv,
    spread_send2,
    spread_recv2,
    local_sem,
    column_send,
    column_recv,
    pair_sem,
    kv_send,
    kv_recv,
    weight_sem,
    small_send,
    small_recv,
    out_send,
    out_recv,
    pair_send,
    pair_recv,
    partial_send,
    partial_recv,
    back_send,
    back_recv,
):
    me = lax.axis_index("wide")
    n = lax.axis_index("narrow")
    core = n % 2
    high = n // 2
    partner = n + 1 - 2 * core
    far = n + 2 - 4 * high
    across = far + 1 - 2 * core
    parity = me % 2
    group = me // KV_SHARE
    mate = me + 1 - 2 * parity

    locals_ = [
        pltpu.make_async_copy(hidden, gathered.at[me], local_sem.at[0]),
        pltpu.make_async_copy(query_weight, joined.at[:, pl.ds(0, LANE)], local_sem.at[1]),
        pltpu.make_async_copy(cache_key.at[group], kv.at[0, 0], local_sem.at[2]),
        pltpu.make_async_copy(cache_value.at[group], kv.at[1, 0], local_sem.at[3]),
        pltpu.make_async_copy(hidden, own_hidden, local_sem.at[4]),
    ]
    for copy in locals_:
        copy.start()
    loads = [
        pltpu.make_async_copy(gate_weight.at[0], gate, weight_sem.at[0]),
        pltpu.make_async_copy(up_weight.at[0], up, weight_sem.at[1]),
        pltpu.make_async_copy(down_weight.at[0], down, weight_sem.at[2]),
    ]

    greet(
        [
            (WIDE - 1, lambda i: ((me + 1 + i) % WIDE, n)),
            (2, lambda i: (me, partner + i * (far - partner))),
            (1, lambda i: (mate, far)),
        ]
    )

    def gather_own():
        locals_[4].wait()
        own = own_hidden[...].astype(F32)
        shift[...] = jnp.broadcast_to(jnp.sum(own, axis=1, keepdims=True) * (1.0 / LANE), (ROWS, LANE))
        own = own - shift[...]
        sums[0] = own
        sums[1] = own * own

    def gather_sums(block, half):
        rows = slice(half * HALF, (half + 1) * HALF)
        moved = gathered[block, rows].astype(F32) - shift[rows]
        sums[0, rows] += moved
        sums[1, rows] += moved * moved

    spread = Spread(hidden, gathered, me, n, spread_send, spread_recv, gather_own, gather_sums)
    spread.start()

    half_rows = pl.ds(core * (LANE // 2), LANE // 2)

    def send_column(i, carry):
        target = flipped(me, i + 1, BITS)
        cut = pl.ds(pl.multiple_of((target // KV_SHARE) * LANE, LANE), LANE)

        @pl.when(target % 2 == 0)
        def _():
            remote(
                key_weight.at[half_rows, cut], columns.at[core, me], column_send.at[0], column_recv.at[0], target, n
            ).start()

        @pl.when(target % 2 == 1)
        def _():
            remote(
                value_weight.at[half_rows, cut], columns.at[core, me], column_send.at[0], column_recv.at[0], target, n
            ).start()

        return carry

    lax.fori_loop(0, WIDE - 1, send_column, 0)
    own_cut = pl.ds(pl.multiple_of(group * LANE, LANE), LANE)

    @pl.when(parity == 0)
    def _():
        pltpu.make_async_copy(key_weight.at[half_rows, own_cut], columns.at[core, me], local_sem.at[5]).start()

    @pl.when(parity == 1)
    def _():
        pltpu.make_async_copy(value_weight.at[half_rows, own_cut], columns.at[core, me], local_sem.at[5]).start()

    spread.run()
    for load in loads:
        load.start()

    wait_bytes(columns.at[core, me], local_sem.at[5])
    wait_bytes(columns.at[0, pl.ds(0, WIDE - 1)], column_recv.at[0])
    swap = remote(columns.at[core], columns.at[core], pair_sem.at[0], pair_sem.at[1], me, partner)
    swap.start()

    def send_out_column(i, carry):
        target = flipped(me, i + 1, BITS)
        cut = pl.ds(pl.multiple_of(target * LANE, LANE), LANE)
        remote(
            out_weight.at[half_rows, cut], out_columns.at[core, me], column_send.at[1], column_recv.at[1], target, n
        ).start()
        return carry

    lax.fori_loop(0, WIDE - 1, send_out_column, 0)
    own_out = pltpu.make_async_copy(
        out_weight.at[half_rows, pl.ds(pl.multiple_of(me * LANE, LANE), LANE)], out_columns.at[core, me], local_sem.at[6]
    )
    own_out.start()

    for copy in locals_[:4]:
        copy.wait()

    swap.wait()
    for half in (0, 1):
        for w in range(WIDE):
            joined[w * LANE + half * (LANE // 2) : w * LANE + (half + 1) * (LANE // 2), LANE:] = columns[half, w]

    def project(tile, carry):
        rows = pl.ds(pl.multiple_of(tile * LANE, LANE), LANE)
        offset = jnp.sum(sums[0, rows], axis=1, keepdims=True) * (1.0 / D)
        square = jnp.sum(sums[1, rows], axis=1, keepdims=True) * (1.0 / D)
        average = jnp.max(shift[rows], axis=1, keepdims=True) + offset
        scale = lax.rsqrt(jnp.maximum(square - offset * offset, 0.0) + EPS)
        for w in range(WIDE):
            centered = gathered[w, rows].astype(F32) - average
            normed[:, w * LANE : (w + 1) * LANE] = (centered * scale * gain[w : w + 1, :]).astype(BF16)
        product = dot(normed[...], joined[...]).astype(BF16)
        queries[rows] = product[:, :LANE]
        kv[parity, n + 1, rows] = product[:, LANE:]
        return carry

    def fresh(kind, block, half):
        return kv.at[kind, block + 1, pl.ds(half * HALF, HALF)]

    def give(kind, half, block, order, wide, narrow):
        piece = fresh(kind, block, half)
        remote(piece, piece, kv_send.at[half, order], kv_recv.at[kind, half, block], wide, narrow).start()

    def take(kind, half, block):
        wait_bytes(fresh(kind, block, half), kv_recv.at[kind, half, block])

    for half in (0, 1):
        lax.fori_loop(half * 2, half * 2 + 2, project, 0)
        give(parity, half, n, 0, mate, n)

        @pl.when(high == 0)
        def _():
            give(parity, half, n, 1, me, far)
            give(parity, half, n, 2, mate, far)

        @pl.when(core == 0)
        def _():
            give(parity, half, n, 3, me, partner)

    row_ids = lax.broadcasted_iota(jnp.int32, (ROWS, ROWS), 0)
    key_ids = lax.broadcasted_iota(jnp.int32, (ROWS, ROWS), 1)
    causal = key_ids <= row_ids

    def attend(j, state):
        highest, total, acc = state
        scores = dot_t(queries[...], kv[0, j]) * SCALE
        scores = jnp.where(jnp.logical_or(causal, j <= n), scores, -1e30)
        new = jnp.maximum(highest, jnp.max(scores, axis=1, keepdims=True))
        weights = jnp.exp(scores - new)
        fade = jnp.exp(highest - new)
        total = total * fade + jnp.sum(weights, axis=1, keepdims=True)
        acc = acc * fade + dot(weights.astype(BF16), kv[1, j])
        return new, total, acc

    state = (
        jnp.full((ROWS, 1), -1e30, F32),
        jnp.zeros((ROWS, 1), F32),
        jnp.zeros((ROWS, LANE), F32),
    )
    state = lax.fori_loop(0, 1, attend, state)
    own_out.wait()
    wait_bytes(out_columns.at[0, pl.ds(0, WIDE - 1)], column_recv.at[1])
    swap_out = remote(out_columns.at[core], out_columns.at[core], pair_sem.at[2], pair_sem.at[3], me, partner)
    swap_out.start()
    for half in (0, 1):
        take(1 - parity, half, n)

        @pl.when(core == 0)
        def _():
            give(1 - parity, half, n, 4, me, partner)

        @pl.when(high == 1)
        def _():
            take(parity, half, far)
            give(parity, half, far, 5, me, partner)
            take(1 - parity, half, far)
            give(1 - parity, half, far, 6, me, partner)

    eye = (
        lax.broadcasted_iota(jnp.int32, (LANE, LANE), 0) == lax.broadcasted_iota(jnp.int32, (LANE, LANE), 1)
    ).astype(F32)

    def to_row(column):
        return jnp.sum(column * eye, axis=0, keepdims=True)

    def to_column(row):
        return jnp.sum(row * eye, axis=1, keepdims=True)

    below = lax.broadcasted_iota(jnp.int32, (LANE, LANE), 0)
    left = lax.broadcasted_iota(jnp.int32, (LANE, LANE), 1)
    earlier = jnp.logical_and(left < below, left // BLOCK == below // BLOCK).astype(BF16)
    expert_ids = lax.broadcasted_iota(jnp.int32, (LANE, EXPERTS), 1)
    slot_ids = lax.broadcasted_iota(jnp.int32, (LANE, EXPERTS * GROUP_SLOTS), 1)
    in_group = lax.broadcasted_iota(jnp.int32, (LANE, 1), 0) // BLOCK * CAP

    def named(g):
        return [
            to_column(ids[k : k + 1, g * LANE : (g + 1) * LANE].astype(F32)).astype(jnp.int32) for k in (0, 1)
        ]

    for g in range(GROUPS):
        pair = named(g)
        hot = [expert_ids == chosen for chosen in pair]
        before = dot(earlier, jnp.logical_or(hot[0], hot[1]).astype(BF16))
        for k in (0, 1):
            position = jnp.sum(jnp.where(hot[k], before, 0.0), axis=1, keepdims=True).astype(jnp.int32)
            slot = pair[k] * GROUP_SLOTS + in_group + position
            placed[g, k] = (slot_ids == slot).astype(BF16)

    swap_out.wait()
    for half in (0, 1):
        for w in range(WIDE):
            out_joined[w * LANE + half * (LANE // 2) : w * LANE + (half + 1) * (LANE // 2), :] = out_columns[half, w]

    for half in (0, 1):

        @pl.when(core == 1)
        def _():
            take(parity, half, partner)
            take(1 - parity, half, partner)

        @pl.when(high == 1)
        def _():
            take(parity, half, across)
            take(1 - parity, half, across)

    _, total, acc = lax.fori_loop(1, n + 2, attend, state)
    attended[...] = (acc / total).astype(BF16)

    def out_rows(block):
        return out_joined[pl.ds(pl.multiple_of(block * LANE, LANE), LANE), :]

    def mix_own():
        mixture[...] = own_hidden[...].astype(F32) + dot(attended[...], out_rows(me))

    def gather_products(block, half):
        rows = slice(half * HALF, (half + 1) * HALF)
        mixture[rows] += dot(mixed[block, rows], out_rows(block))

    spread2 = Spread(attended, mixed, me, n, spread_send2, spread_recv2, mix_own, gather_products)
    spread2.start()

    spread2.run()

    def dispatch(part):
        groups = pl.ds(*PARTS[part])
        slot = arrived.at[n * WIDE + me, groups]

        def one(i, carry):
            target = flipped(me, i, BITS)
            source = outgoing.at[target // 2, groups]

            @pl.when(i > 0)
            def _():
                remote(source, slot, out_send.at[part], out_recv.at[part, high], target, n).start()

            remote(source, slot, out_send.at[part], out_recv.at[part, high], target, far).start()
            return carry

        lax.fori_loop(0, WIDE, one, 0)
        pltpu.make_async_copy(outgoing.at[me // 2, groups], slot, local_sem.at[8 + part]).start()

    def share(mine, everyone, which):
        def one(i, carry):
            target = flipped(me, i + 1, BITS)
            remote(mine, everyone.at[me], small_send.at[which], small_recv.at[which], target, n).start()
            return carry

        lax.fori_loop(0, WIDE - 1, one, 0)

    def collect(mine, everyone, which):
        everyone[me] = mine[...]
        wait_bytes(everyone.at[pl.ds(0, WIDE - 1)], small_recv.at[which])

    def deviations_of(g):
        values = residual[g * LANE : (g + 1) * LANE].astype(F32)
        average = jnp.sum(values, axis=1, keepdims=True) * (1.0 / LANE)
        centered = values - average
        deviations = jnp.sum(centered * centered, axis=1, keepdims=True)
        stats[g : g + 1, :] = to_row(average)
        stats[GROUPS + g : GROUPS + g + 1, :] = to_row(deviations)

    for part, (first_group, count) in enumerate(PARTS):
        for g in range(first_group, first_group + count):
            rows = slice(g * LANE, (g + 1) * LANE)
            here = mixture[rows].astype(BF16)
            residual[rows] = here
            filled = lax.dot_general(
                placed[g, 0] + placed[g, 1], here, (((0,), (0,)), ((), ())), preferred_element_type=F32
            ).astype(BF16)
            outgoing[:, g] = filled.reshape(EXPERTS, GROUP_SLOTS, LANE)
        dispatch(part)
        if part == 0:
            for g in range(GROUPS):
                residual[g * LANE : (g + 1) * LANE] = mixture[g * LANE : (g + 1) * LANE].astype(BF16)
                deviations_of(g)
            share(stats, stats_in, 0)

    def norm_tokens(part, source):
        first_group, count = PARTS[part]
        size = count * GROUP_SLOTS

        def values(w):
            block = arrived[source * WIDE + w, first_group : first_group + count]
            return block.reshape(size, LANE).astype(F32)

        total = jnp.zeros((size, LANE), F32)
        for w in range(WIDE):
            total += values(w)
        average = jnp.sum(total, axis=1, keepdims=True) * (1.0 / D)
        total = jnp.zeros((size, LANE), F32)
        for w in range(WIDE):
            centered = values(w) - average
            total += centered * centered
        scale = lax.rsqrt(jnp.sum(total, axis=1, keepdims=True) * (1.0 / D) + EPS)
        where = pl.ds(pl.multiple_of(((source % 2) * 2 + source // 2) * size, GROUP_SLOTS), size)
        for w in range(WIDE):
            centered = values(w) - average
            tokens[where, w * LANE : (w + 1) * LANE] = (centered * scale * gain_two[w : w + 1, :]).astype(BF16)

    swaps = []

    def receive(part):
        groups = pl.ds(*PARTS[part])
        wait_bytes(outgoing.at[0, groups], local_sem.at[8 + part])
        for order, where in enumerate((high, 1 - high)):
            blocks = WIDE - 1 if order == 0 else WIDE
            wait_bytes(arrived.at[pl.ds(0, blocks), groups], out_recv.at[part, where])
            piece = arrived.at[pl.ds((where * 2 + core) * WIDE, WIDE), groups]
            swap = remote(piece, piece, pair_send.at[part, where], pair_recv.at[part, where], me, partner)
            swap.start()
            swaps.append(swap)

    def experts(part):
        first_group, count = PARTS[part]
        groups = pl.ds(first_group, count)
        size = count * GROUP_SLOTS
        rows = count * OWN
        everything = pl.ds(0, 2 * rows)
        for where in (0, 1):
            norm_tokens(part, where * 2 + core)
        for where in (0, 1):
            wait_bytes(arrived.at[pl.ds(0, WIDE), groups], pair_recv.at[part, where])
            norm_tokens(part, where * 2 + 1 - core)
        gated = dot_t(tokens[everything], gate[...])
        raised = dot_t(tokens[everything], up[...])
        active[everything] = (gated / (1.0 + jnp.exp(-gated)) * raised).astype(BF16)
        if part + 1 < len(PARTS):
            receive(part + 1)

        def step(k, carry):
            @pl.when(k < STEPS)
            def _():
                block = flipped(me // 4, k, 3)
                cut = pl.ds(pl.multiple_of(block * COLS, COLS), COLS)
                total = dot(active[everything], down[:, cut])
                at = pl.ds(first_group * STEPS + k * count, count)

                @pl.when(core == 0)
                def _():
                    kept[k, :rows] = total[:rows]
                    partial_out[at] = total[rows:].astype(BF16).reshape(count, OWN, COLS)

                @pl.when(core == 1)
                def _():
                    kept[k, :rows] = total[rows:]
                    partial_out[at] = total[:rows].astype(BF16).reshape(count, OWN, COLS)

                sem = part * STEPS + k
                remote(
                    partial_out.at[at], partial_in.at[at], partial_send.at[sem], partial_recv.at[sem], me, partner
                ).start()

            @pl.when(k >= LAG)
            def _():
                late = k - LAG
                block = flipped(me // 4, late, 3)
                at = pl.ds(first_group * STEPS + late * count, count)
                wait_bytes(partial_in.at[at], partial_recv.at[part * STEPS + late])
                other = partial_in[at].reshape(rows, COLS).astype(F32)
                total = (kept[late, :rows] + other).astype(BF16)
                base = block * 4
                for where in (0, 1):
                    for q in range(4):
                        returning[base + where * WIDE + q, first_group : first_group + count] = total[
                            where * size : (where + 1) * size, q * LANE : (q + 1) * LANE
                        ].reshape(count, GROUP_SLOTS, LANE)
                for q in range(4):
                    spot = flipped(me % 4, q, 2)
                    target = block * 4 + spot
                    for turn in (0, 1):
                        where = high if turn == 0 else 1 - high
                        slot = returning.at[base + where * WIDE + spot, groups]
                        home = returned.at[high * WIDE + me, groups]
                        sems = back_send.at[part], back_recv.at[part, high]
                        if turn == 1 or q > 0:
                            remote(slot, home, *sems, target, where * 2 + core).start()
                        else:

                            @pl.when(late > 0)
                            def _():
                                remote(slot, home, *sems, target, where * 2 + core).start()

                            @pl.when(late == 0)
                            def _():
                                pltpu.make_async_copy(slot, home, local_sem.at[11 + part]).start()

            return carry

        lax.fori_loop(0, STEPS + LAG, step, 0)

    def combine(part):
        first_group, count = PARTS[part]
        groups = pl.ds(first_group, count)
        wait_bytes(returned.at[0, groups], local_sem.at[11 + part])
        wait_bytes(returned.at[pl.ds(0, WIDE - 1), groups], back_recv.at[part, high])
        wait_bytes(returned.at[pl.ds(0, WIDE), groups], back_recv.at[part, 1 - high])
        for g in range(first_group, first_group + count):
            picks = [jnp.zeros((LANE, LANE), F32)] * 2
            for where in (0, 1):
                for s in (0, 1):
                    rows = jnp.concatenate([returned[where * WIDE + 2 * e + s, g] for e in range(EXPERTS)], axis=0)
                    picks = [picks[k] + dot(placed[g, k], rows) for k in (0, 1)]
            weight = to_column(heavy[g : g + 1])
            result[g * LANE : (g + 1) * LANE] = (
                residual[g * LANE : (g + 1) * LANE].astype(F32) + weight * picks[0] + (1.0 - weight) * picks[1]
            ).astype(BF16)

    receive(0)
    for load in loads:
        load.wait()
    experts(0)
    experts(1)

    collect(stats, stats_in, 0)
    averages = jnp.zeros((GROUPS, LANE), F32)
    for w in range(WIDE):
        averages += stats_in[w, :GROUPS]
    averages = averages * (1.0 / WIDE)
    squares = jnp.zeros((GROUPS, LANE), F32)
    for w in range(WIDE):
        shift = stats_in[w, :GROUPS] - averages
        squares += stats_in[w, GROUPS:] + LANE * (shift * shift)
    scales = lax.rsqrt(squares * (1.0 / D) + EPS)
    own_gain = gain_two[pl.ds(me, 1), :]
    own_router = router[:, pl.ds(pl.multiple_of(me * LANE, LANE), LANE)]
    for g in range(GROUPS):
        values = residual[g * LANE : (g + 1) * LANE].astype(F32)
        here = ((values - to_column(averages[g : g + 1])) * to_column(scales[g : g + 1]) * own_gain).astype(BF16)
        logits = dot_t(here, own_router)
        pair = named(g)
        lead = jnp.sum(
            jnp.where(expert_ids == pair[0], logits, 0.0) - jnp.where(expert_ids == pair[1], logits, 0.0),
            axis=1,
            keepdims=True,
        )
        diffs[g : g + 1, :] = to_row(lead)
        diffs[GROUPS + g : GROUPS + g + 1, :] = jnp.zeros((1, LANE), F32)
    share(diffs, diffs_in, 1)
    experts(2)

    collect(diffs, diffs_in, 1)
    leads = jnp.zeros((GROUPS, LANE), F32)
    for w in range(WIDE):
        leads += diffs_in[w, :GROUPS]
    heavy = 1.0 / (1.0 + jnp.exp(-leads))
    for part in range(len(PARTS)):
        combine(part)

    spread.finish()
    spread2.finish()
    for swap in swaps:
        swap.wait_send()
    for which in range(2):
        wait_bytes(columns.at[0, pl.ds(0, WIDE - 1)], column_send.at[which])
        wait_bytes(stats_in.at[pl.ds(0, WIDE - 1)], small_send.at[which])
    for half in (0, 1):

        def sent(order, half=half):
            wait_bytes(fresh(parity, n, half), kv_send.at[half, order])

        sent(0)

        @pl.when(high == 0)
        def _():
            sent(1)
            sent(2)

        @pl.when(core == 0)
        def _():
            sent(3)
            sent(4)

        @pl.when(high == 1)
        def _():
            sent(5)
            sent(6)

    for part, (first_group, count) in enumerate(PARTS):
        groups = pl.ds(first_group, count)
        wait_bytes(arrived.at[pl.ds(0, 2 * WIDE - 1), groups], out_send.at[part])
        wait_bytes(returned.at[pl.ds(0, 2 * WIDE - 1), groups], back_send.at[part])
        for k in range(STEPS):
            wait_bytes(partial_out.at[pl.ds(0, count)], partial_send.at[part * STEPS + k])


def body(
    hidden,
    attn_gain,
    query_weight,
    key_weight,
    value_weight,
    out_weight,
    cache_key,
    cache_value,
    mlp_gain,
    router_weight,
    expert_ids,
    gate_weight,
    up_weight,
    down_weight,
):
    anywhere = pl.BlockSpec(memory_space=pl.ANY)
    vmem = pl.BlockSpec(memory_space=pltpu.VMEM)
    dma = pltpu.SemaphoreType.DMA

    def held(*shape, kind=BF16):
        return pltpu.VMEM(shape, kind)

    return pl.pallas_call(
        layer_kernel,
        out_shape=jax.ShapeDtypeStruct((ROWS, LANE), BF16),
        in_specs=[anywhere, vmem] + [anywhere] * 6 + [vmem] * 3 + [anywhere] * 3,
        out_specs=vmem,
        scratch_shapes=[
            held(WIDE, ROWS, LANE),
            held(WIDE, ROWS, LANE),
            held(LANE, D),
            held(D, 2 * LANE),
            held(2, WIDE, LANE // 2, LANE),
            held(2, WIDE, LANE // 2, LANE),
            held(D, LANE),
            held(2, NARROW + 1, ROWS, LANE),
            held(ROWS, LANE),
            held(ROWS, LANE),
            held(ROWS, LANE),
            held(ROWS, LANE),
            held(ROWS, LANE, kind=F32),
            held(2, ROWS, LANE, kind=F32),
            held(ROWS, LANE, kind=F32),
            held(HIDDEN, D),
            held(HIDDEN, D),
            held(HIDDEN, D),
            held(2 * GROUPS, LANE, kind=F32),
            held(WIDE, 2 * GROUPS, LANE, kind=F32),
            held(2 * GROUPS, LANE, kind=F32),
            held(WIDE, 2 * GROUPS, LANE, kind=F32),
            held(GROUPS, 2, LANE, EXPERTS * GROUP_SLOTS),
            held(EXPERTS, GROUPS, GROUP_SLOTS, LANE),
            held(ALL, GROUPS, GROUP_SLOTS, LANE),
            held(2 * LANE, D),
            held(2 * LANE, HIDDEN),
            held(GROUPS * STEPS, OWN, COLS),
            held(GROUPS * STEPS, OWN, COLS),
            held(STEPS, LANE, COLS, kind=F32),
            held(2 * WIDE, GROUPS, GROUP_SLOTS, LANE),
            held(2 * WIDE, GROUPS, GROUP_SLOTS, LANE),
            dma((SENDS,)),
            dma((2, WIDE)),
            dma((SENDS,)),
            dma((2, WIDE)),
            dma((11 + len(PARTS),)),
            dma((2,)),
            dma((2,)),
            dma((4,)),
            dma((2, 7)),
            dma((2, 2, NARROW)),
            dma((3,)),
            dma((2,)),
            dma((2,)),
            dma((len(PARTS),)),
            dma((len(PARTS), 2)),
            dma((len(PARTS), 2)),
            dma((len(PARTS), 2)),
            dma((len(PARTS) * STEPS,)),
            dma((len(PARTS) * STEPS,)),
            dma((len(PARTS),)),
            dma((len(PARTS), 2)),
        ],
        compiler_params=pltpu.CompilerParams(
            collective_id=0, has_side_effects=True, vmem_limit_bytes=60 * 2**20
        ),
    )(
        hidden,
        attn_gain.reshape(WIDE, LANE),
        query_weight,
        key_weight,
        value_weight,
        out_weight,
        cache_key,
        cache_value,
        mlp_gain.reshape(WIDE, LANE),
        router_weight.T,
        expert_ids.T,
        gate_weight.swapaxes(1, 2),
        up_weight.swapaxes(1, 2),
        down_weight,
    )


def solution(mesh):
    placed = (
        P("narrow", "wide"),
        P(),
        P(None, "wide"),
        P("wide", None),
        P("wide", None),
        P("wide", None),
        P(),
        P(),
        P(),
        P(),
        P("narrow", None),
        P("wide", None, "narrow"),
        P("wide", None, "narrow"),
        P("wide", "narrow", None),
    )
    return jax.shard_map(
        body, mesh=mesh, in_specs=placed, out_specs=P("narrow", "wide"), check_vma=False
    )
```
